32 devices in a mesh: section: 2 (over core), dp: 16 (over z, y, x).
Axes of the slice: x: 2, y: 2, z: 4, core: 2. Of those that a mesh axis runs over, the one named last changes fastest.
Arguments:
- activations: bfloat16 [256, 256, 384], P('dp'), may hold values from -6 to 6
- cotangent: bfloat16 [256, 256, 384], P('dp'), may hold values from -6 to 6
- segment_ids: int32 [256, 256], P('dp'), may hold values from 0 to 5, as said below
- pad_mask: int32 [256, 256], P('dp'), may hold values from 0 to 1, as said below
- norm1_gain: float32 [2, 384], P('section'), may hold values from 0.1 to 1.9
- norm1_bias: float32 [2, 384], P('section'), may hold values from -4 to 4
- qkv_weight: bfloat16 [2, 384, 1152], P('section'), may hold values from -0.4375 to 0.4375
- qv_bias: float32 [2, 768], P('section'), may hold values from -6 to 6
- out_weight: bfloat16 [2, 384, 384], P('section'), may hold values from -0.875 to 0.875
- out_bias: float32 [2, 384], P('section'), may hold values from -4 to 4
- norm2_gain: float32 [2, 384], P('section'), may hold values from 0.1 to 1.9
- norm2_bias: float32 [2, 384], P('section'), may hold values from -4 to 4
- up_weight: bfloat16 [2, 384, 1536], P('section'), may hold values from -0.3125 to 0.3125
- up_bias: float32 [2, 1536], P('section'), may hold values from -4 to 4
- down_weight: bfloat16 [2, 1536, 384], P('section'), may hold values from -0.15625 to 0.15625
- down_bias: float32 [2, 384], P('section'), may hold values from -4 to 4
Outputs:
- layer_outs: bfloat16 [2, 256, 256, 384], P('section', 'dp')
- layer_in_grads: float32 [2, 256, 256, 384], P('section', 'dp')
- norm1_gain_grad: float32 [2, 384], P('section')
- norm1_bias_grad: float32 [2, 384], P('section')
- qkv_weight_grad: float32 [2, 384, 1152], P('section')
- qv_bias_grad: float32 [2, 768], P('section')
- out_weight_grad: float32 [2, 384, 384], P('section')
- out_bias_grad: float32 [2, 384], P('section')
- norm2_gain_grad: float32 [2, 384], P('section')
- norm2_bias_grad: float32 [2, 384], P('section')
- up_weight_grad: float32 [2, 384, 1536], P('section')
- up_bias_grad: float32 [2, 1536], P('section')
- down_weight_grad: float32 [2, 1536, 384], P('section')
- down_bias_grad: float32 [2, 384], P('section')
The draws below stay inside these ranges and needn't reach their ends.
Inputs may be any that keep to these rules, and one draw needn't show every extreme that they name: `segment_ids`: each row is packed from its start with whole segments of 37 slots or of 85 to 192 slots; ids start at 0 and rise by one at each new segment; padding slots carry the id of the row's last segment. Some row of every draw holds only segments of 37 slots and reaches the largest id. `pad_mask`: in each row the slots holding patches come first and padding fills the rest; the first 37 slots of a row are always 1.
All inputs are finite; a program needn't handle non-finite values.
Results may differ from the reference program's by a relative error of at most 0.03.
Values may be sent and summed in bfloat16 or wider, within the bound.
No kernel may reach another device: no remote copies, remote signals or barrier semaphores. Data moves between devices by JAX's collectives and lax.ppermute only.
A program may use at most 256 MiB of HBM per device.

```python
import jax
import jax.numpy as jnp
from jax import lax

D = 384
H = 6
DH = 64
FF = 1536
S = 256
ROWS_DEV = 16
ROWS = 256
N_DP = 16


def packing(key):
    view_kinds = jax.random.randint(jax.random.fold_in(key, 101), (ROWS, 8), 0, 2)
    short_row = jax.random.randint(jax.random.fold_in(key, 103), (), 0, ROWS)
    rows_index = jnp.arange(ROWS, dtype=jnp.int32)
    view_kinds = jnp.where(rows_index[:, None] == short_row, 0, view_kinds)
    kept_counts = jax.random.randint(jax.random.fold_in(key, 102), (ROWS, 8), S // 3, 3 * S // 4 + 1)
    lengths = jnp.where(view_kinds > 0, kept_counts, S // 7 + 1)
    return jnp.cumsum(lengths, axis=1).astype(jnp.int32)


def draw_segment_ids(key, part):
    segment_ends = packing(key)
    positions = jnp.arange(S, dtype=jnp.int32)
    crossed = jnp.sum((segment_ends[:, None, :] <= positions[None, :, None]).astype(jnp.int32), axis=-1)
    fitted = jnp.sum((segment_ends <= S).astype(jnp.int32), axis=1)
    return jnp.minimum(crossed, fitted[:, None] - 1).astype(jnp.int32)


def draw_pad_mask(key, part):
    segment_ends = packing(key)
    positions = jnp.arange(S, dtype=jnp.int32)
    used_slots = jnp.max(jnp.where(segment_ends <= S, segment_ends, 0), axis=1)
    return (positions[None, :] < used_slots[:, None]).astype(jnp.int32)


def levels(key, extent, split, least, top_value):
    def one(dim, parts):
        steps = jax.random.uniform(jax.random.fold_in(jax.random.fold_in(key, 6), dim), (parts,), jnp.float32, least / len(split), top_value / len(split))
        return jnp.repeat(jnp.exp(steps), extent[dim] // parts).reshape((-1,) + (1,) * (len(extent) - dim - 1))

    factor_of = one(*split[0])
    for cut in split[1:]:
        factor_of = factor_of * one(*cut)
    return factor_of


def scatter_about(rng, dims, scale, bound, split=(), kind=jnp.bfloat16):
    result = scale * jax.random.normal(rng, dims, jnp.float32)
    if split:
        result = result * levels(rng, dims, split, -0.22, 0.18)
    return jnp.clip(result, -bound, bound).astype(kind)


def setup_inputs(seed: int = 0) -> dict:
    key_of = jax.random.split(jax.random.key(seed), 17)
    return {
        "activations": scatter_about(key_of[0], (ROWS, S, D), 1.0, 6.0, ((0, 16),)),
        "cotangent": scatter_about(key_of[1], (ROWS, S, D), 1.0, 6.0, ((0, 16),)),
        "segment_ids": draw_segment_ids(jax.random.fold_in(key_of[16], 71), 0),
        "pad_mask": draw_pad_mask(jax.random.fold_in(key_of[16], 71), 0),
        "norm1_gain": jnp.clip(1.0 + 0.18 * jax.random.normal(key_of[4], (2, D), jnp.float32), 0.1, 1.9),
        "norm1_bias": scatter_about(key_of[5], (2, D), 0.3, 4.0, ((0, 2),), jnp.float32),
        "qkv_weight": scatter_about(key_of[6], (2, D, 3 * D), (D // 2) ** -0.5, 0.4375, ((0, 2),)),
        "qv_bias": scatter_about(key_of[7], (2, 2 * D), 0.5, 6.0, ((0, 2),), jnp.float32),
        "out_weight": scatter_about(key_of[8], (2, D, D), (D // 8) ** -0.5, 0.875, ((0, 2),)),
        "out_bias": scatter_about(key_of[9], (2, D), 0.3, 4.0, ((0, 2),), jnp.float32),
        "norm2_gain": jnp.clip(1.0 + 0.18 * jax.random.normal(key_of[10], (2, D), jnp.float32), 0.1, 1.9),
        "norm2_bias": scatter_about(key_of[11], (2, D), 0.3, 4.0, ((0, 2),), jnp.float32),
        "up_weight": scatter_about(key_of[12], (2, D, FF), D ** -0.5, 0.3125, ((0, 2),)),
        "up_bias": scatter_about(key_of[13], (2, FF), 0.3, 4.0, ((0, 2),), jnp.float32),
        "down_weight": scatter_about(key_of[14], (2, FF, D), FF ** -0.5, 0.15625, ((0, 2),)),
        "down_bias": scatter_about(key_of[15], (2, D), 0.3, 4.0, ((0, 2),), jnp.float32),
    }


@jax.custom_vjp
def low(v):
    return lax.optimization_barrier(v.astype(jnp.bfloat16)).astype(jnp.float32)

@jax.custom_vjp
def low_back(v):
    return v

def low_keep(v):
    return (low(v), None)

def low_pass(kept, grad):
    return (grad,)

def back_keep(v):
    return (v, None)

def back_low(kept, grad):
    return (low(grad),)
low.defvjp(low_keep, low_pass)
low_back.defvjp(back_keep, back_low)
highest = lax.Precision.HIGHEST
norm_eps = 1e-06
sqrt_half = 0.7071067811865476

def layer_norm(inputs, norm_gain, norm_shift):
    average = lax.optimization_barrier(jnp.mean(inputs, axis=-1, keepdims=True))
    centred = inputs - average
    spread = lax.optimization_barrier(jnp.mean(centred * centred, axis=-1, keepdims=True))
    return centred * lax.rsqrt(spread + norm_eps) * norm_gain + norm_shift

def attention(queries, key_heads, value_heads, segments, valid_slots):
    scores = jnp.einsum('rqhd,rkhd->rhqk', queries, key_heads, precision=highest) * DH ** (-0.5)
    scores = low_back(scores)
    allowed = (segments[:, :, None] == segments[:, None, :]) & (valid_slots[:, None, :] > 0)
    scores = jnp.where(allowed[:, None, :, :], scores, -1e+30)
    top_score = lax.optimization_barrier(jnp.max(scores, axis=-1, keepdims=True))
    weights = jnp.exp(scores - top_score)
    attn_probs = low(weights / lax.optimization_barrier(jnp.sum(weights, axis=-1, keepdims=True)))
    return jnp.einsum('rhqk,rkhd->rqhd', attn_probs, value_heads, precision=highest)

def block_layer(inputs, params, segments, valid_slots):
    gain_attn, shift_attn, qkv_matrix, qv_offset, out_matrix, out_offset, gain_mlp, shift_mlp, up_matrix, up_offset, down_matrix, down_offset = params
    batch_rows = inputs.shape[0]
    normed = low(layer_norm(inputs, gain_attn, shift_attn))
    offsets = jnp.concatenate([qv_offset[:D], jnp.zeros((D,), jnp.float32), qv_offset[D:]])
    projected = jnp.einsum('rsd,de->rse', normed, qkv_matrix, precision=highest) + offsets
    projected = low_back(low(projected))
    queries = projected[:, :, :D].reshape(batch_rows, S, H, DH)
    key_heads = projected[:, :, D:2 * D].reshape(batch_rows, S, H, DH)
    value_heads = projected[:, :, 2 * D:].reshape(batch_rows, S, H, DH)
    mixed_heads = attention(queries, key_heads, value_heads, segments, valid_slots)
    mixed_low = low_back(low(mixed_heads.reshape(batch_rows, S, D)))
    branch = low_back(jnp.einsum('rsd,de->rse', mixed_low, out_matrix, precision=highest) + out_offset)
    residual = inputs + branch
    normed_mlp = low(layer_norm(residual, gain_mlp, shift_mlp))
    hidden = jnp.einsum('rsd,df->rsf', normed_mlp, up_matrix, precision=highest) + up_offset
    hidden = low_back(hidden)
    activated = low(hidden * 0.5 * (1.0 + lax.erf(hidden * sqrt_half)))
    outcome = low_back(jnp.einsum('rsf,fd->rsd', activated, down_matrix, precision=highest) + down_offset)
    return valid_slots[:, :, None] * (residual + outcome)

def two_layers(inputs, first_params, second_params, probe, segments, valid_slots):
    first_out = low(block_layer(inputs, first_params, segments, valid_slots))
    second_in = low_back(first_out) + probe
    second_out = low(block_layer(second_in, second_params, segments, valid_slots))
    return (first_out, second_out)

def reference(activations, cotangent, segment_ids, pad_mask, norm1_gain, norm1_bias, qkv_weight, qv_bias, out_weight, out_bias, norm2_gain, norm2_bias, up_weight, up_bias, down_weight, down_bias):
    stacked = (norm1_gain, norm1_bias, qkv_weight.astype(jnp.float32), qv_bias, out_weight.astype(jnp.float32), out_bias, norm2_gain, norm2_bias, up_weight.astype(jnp.float32), up_bias, down_weight.astype(jnp.float32), down_bias)
    first_params = tuple((tensor[0] for tensor in stacked))
    second_params = tuple((tensor[1] for tensor in stacked))
    group_inputs = activations.astype(jnp.float32).reshape(N_DP, ROWS_DEV, S, D)
    group_seeds = cotangent.astype(jnp.float32).reshape(N_DP, ROWS_DEV, S, D)
    group_segments = segment_ids.reshape(N_DP, ROWS_DEV, S)
    group_valid = pad_mask.reshape(N_DP, ROWS_DEV, S)

    def group_step(totals, pieces):
        inputs, seed_rows, segments, valid_int = pieces
        valid_slots = valid_int.astype(jnp.float32)

        def forward(inputs_in, params_one, params_two, probe_in):
            return two_layers(inputs_in, params_one, params_two, probe_in, segments, valid_slots)
        outputs, pullback = jax.vjp(forward, inputs, first_params, second_params, jnp.zeros_like(inputs))
        grad_in, grad_first, grad_second, grad_probe = pullback((jnp.zeros_like(outputs[0]), seed_rows))
        totals = jax.tree.map(jnp.add, totals, (grad_first, grad_second))
        return (totals, (outputs[0].astype(jnp.bfloat16), outputs[1].astype(jnp.bfloat16), grad_in, grad_probe))
    initial = jax.tree.map(jnp.zeros_like, (first_params, second_params))
    totals, stacked_out = lax.scan(group_step, initial, (group_inputs, group_seeds, group_segments, group_valid))
    first_out, second_out, first_grad, second_grad = stacked_out
    layer_outs = jnp.stack([first_out.reshape(ROWS, S, D), second_out.reshape(ROWS, S, D)])
    layer_in_grads = jnp.stack([first_grad.reshape(ROWS, S, D), second_grad.reshape(ROWS, S, D)])
    gradients = [jnp.stack([first_part, second_part]) for first_part, second_part in zip(totals[0], totals[1])]
    norm1_gain_grad, norm1_bias_grad, qkv_weight_grad, qv_bias_grad, out_weight_grad, out_bias_grad, norm2_gain_grad, norm2_bias_grad, up_weight_grad, up_bias_grad, down_weight_grad, down_bias_grad = gradients
    return (layer_outs, layer_in_grads, norm1_gain_grad, norm1_bias_grad, qkv_weight_grad, qv_bias_grad, out_weight_grad, out_bias_grad, norm2_gain_grad, norm2_bias_grad, up_weight_grad, up_bias_grad, down_weight_grad, down_bias_grad)
```

```python
import functools

import jax
import jax.numpy as jnp
from jax import lax
from jax.experimental import pallas as pl
from jax.experimental.pallas import tpu as pltpu
from jax.sharding import PartitionSpec as P

H = 6
R = 2
BLOCK = 128
SMALL_ROWS = 256
norm_eps = 1e-06
forbidden = -1e30
sqrt_half = 0.7071067811865476
inverse_root_two_pi = 0.3989422804014327
VMEM_LIMIT = 60 * 1024 * 1024
low = jnp.bfloat16
full = jnp.float32


def nn(a, b):
    return lax.dot_general(a, b, (((1,), (0,)), ((), ())), preferred_element_type=full)


def nt(a, b):
    return lax.dot_general(a, b, (((1,), (1,)), ((), ())), preferred_element_type=full)


def tn(a, b):
    return lax.dot_general(a, b, (((0,), (0,)), ((), ())), preferred_element_type=full)


def column_blocks(width, step):
    return [(start, min(start + step, width)) for start in range(0, width, step)]


def fold_rows(values):
    return jnp.sum(values.reshape(values.shape[0] // 8, 8, values.shape[1]), axis=0)


def gelu_parts(hidden):
    size = jnp.abs(hidden)
    t = pl.reciprocal(1.0 + (0.3275911 * sqrt_half) * size, approx=True)
    bell = jnp.exp(-0.5 * (hidden * hidden))
    series = t * (
        0.127414796
        + t * (-0.142248368 + t * (0.7107068705 + t * (-0.7265760135 + t * 0.5307027145)))
    )
    tail = series * bell
    cdf = jnp.where(hidden >= 0.0, 1.0 - tail, tail)
    return (hidden * cdf, cdf + (hidden * inverse_root_two_pi) * bell)


def norm_parts(values):
    average = jnp.mean(values, axis=-1, keepdims=True)
    centred = values - average
    inverse = lax.rsqrt(jnp.mean(centred * centred, axis=-1, keepdims=True) + norm_eps)
    return (centred * inverse, inverse)


def head_lanes():
    lane = lax.broadcasted_iota(jnp.int32, (1, BLOCK), 1)
    first = jnp.where(lane < BLOCK // 2, 1.0, 0.0)
    return (first.astype(low), (1.0 - first).astype(low))


def fetch_weights(section_ref, layer, own, other, held, sems):
    @pl.when(pl.program_id(0) == 0)
    def _():
        @pl.when(section_ref[0] == layer)
        def _():
            for i in range(len(own)):
                pltpu.make_async_copy(own[i], held[i], sems.at[i]).start()

        @pl.when(section_ref[0] != layer)
        def _():
            for i in range(len(own)):
                pltpu.make_async_copy(other[i], held[i], sems.at[i]).start()

        for i in range(len(own)):
            pltpu.make_async_copy(own[i], held[i], sems.at[i]).wait()


def forward_kernel(
    layer,
    slots,
    section_ref,
    x_ref,
    segment_ref,
    block_ref,
    valid_ref,
    vec1_ref,
    vecup_ref,
    *rest,
):
    own, other = rest[0:4], rest[4:8]
    out_ref, qkv_ref, e_ref, rinv_ref, mixed_ref, xhat_ref, inv_ref, act_ref, slope_ref = rest[8:17]
    wqkv, wout, wup, wdown, na_s, res_s, nb_s, sems = rest[17:]
    fetch_weights(section_ref, layer, own, other, (wqkv, wout, wup, wdown), sems)
    tokens, width = x_ref.shape
    hidden_width = wup.shape[1]
    step = 64
    gain_a, shift_a = vec1_ref[0:1, :], vec1_ref[1:2, :]
    q_off, v_off = vec1_ref[2:3, :], vec1_ref[3:4, :]
    out_off, gain_b, shift_b, down_off = (vec1_ref[i : i + 1, :] for i in range(4, 8))
    for t in range(0, tokens, step):
        scaled, _ = norm_parts(x_ref[t : t + step, :].astype(full))
        na_s[t : t + step, :] = (scaled * gain_a + shift_a).astype(low)
    for n0, n1 in column_blocks(3 * width, 512):
        part = nn(na_s[...], wqkv[:, n0:n1])
        for c in range(n0, n1, BLOCK):
            piece = part[:, c - n0 : c - n0 + BLOCK]
            if c < width:
                piece = (piece + q_off[:, c : c + BLOCK]) * 0.125
            elif c >= 2 * width:
                piece = piece + v_off[:, c - 2 * width : c - 2 * width + BLOCK]
            qkv_ref[:, c : c + BLOCK] = piece.astype(low)
    lanes = head_lanes()
    ones = jnp.ones((slots, BLOCK), low)
    for r in range(tokens // slots):
        rows = slice(r * slots, (r + 1) * slots)
        for p in range(H // 2):
            q2 = qkv_ref[rows, p * BLOCK : (p + 1) * BLOCK]
            k2 = qkv_ref[rows, width + p * BLOCK : width + (p + 1) * BLOCK]
            v2 = qkv_ref[rows, 2 * width + p * BLOCK : 2 * width + (p + 1) * BLOCK]
            keys = jnp.concatenate([k2, block_ref[rows, :]], axis=1)
            weights = []
            for i in range(2):
                queries = jnp.concatenate([q2 * lanes[i], segment_ref[rows, :]], axis=1)
                scores = nt(queries, keys)
                e = jnp.exp(scores - jnp.max(scores, axis=1, keepdims=True)).astype(low)
                e_ref[rows, (2 * p + i) * slots : (2 * p + i + 1) * slots] = e
                weights.append(e)
            values = jnp.concatenate(
                [
                    jnp.concatenate([v2 * lanes[0], ones * lanes[0]], axis=1),
                    jnp.concatenate([v2 * lanes[1], ones * lanes[1]], axis=1),
                ],
                axis=0,
            )
            both = nn(jnp.concatenate(weights, axis=1), values)
            rinv = 1.0 / both[:, BLOCK:]
            rinv_ref[rows, p * BLOCK : (p + 1) * BLOCK] = rinv
            mixed_ref[rows, p * BLOCK : (p + 1) * BLOCK] = (both[:, :BLOCK] * rinv).astype(low)
    res_s[...] = x_ref[...].astype(full) + (nn(mixed_ref[...], wout[...]) + out_off)
    for t in range(0, tokens, step):
        scaled, inverse = norm_parts(res_s[t : t + step, :])
        xhat_ref[t : t + step, :] = scaled.astype(low)
        inv_ref[t : t + step, :] = jnp.broadcast_to(inverse, (step, BLOCK))
        nb_s[t : t + step, :] = (scaled * gain_b + shift_b).astype(low)
    for n0, n1 in column_blocks(hidden_width, 256):
        hidden = nn(nb_s[...], wup[:, n0:n1]) + vecup_ref[0:1, n0:n1]
        act, slope = gelu_parts(hidden)
        act_ref[:, n0:n1] = act.astype(low)
        slope_ref[:, n0:n1] = slope.astype(low)
    outcome = res_s[...] + (nn(act_ref[...], wdown[...]) + down_off)
    for c in range(0, width, BLOCK):
        out_ref[:, c : c + BLOCK] = (
            valid_ref[...].astype(full) * outcome[:, c : c + BLOCK]
        ).astype(low)


def store_small(pay_ref, base, vectors):
    row = jnp.concatenate([jnp.sum(v, axis=0, keepdims=True) for v in vectors], axis=1)
    count = row.shape[1] // BLOCK
    pieces = [row[:, j * BLOCK : (j + 1) * BLOCK] for j in range(count)]
    padded = -(-count // 16) * 16
    pieces.append(jnp.zeros((padded - count, BLOCK), full))
    block = jnp.concatenate(pieces, axis=0).astype(low)
    rest = jnp.zeros((SMALL_ROWS - padded, BLOCK), low)
    for h in range(2):
        pay_ref[h, base : base + padded, :] = block
        pay_ref[h, base + padded : base + SMALL_ROWS, :] = rest


def ffn_backward_kernel(
    layer,
    section_ref,
    dy_ref,
    valid_ref,
    xhat_ref,
    inv_ref,
    act_ref,
    slope_ref,
    vec1_ref,
    *rest,
):
    own, other = rest[0:2], rest[2:4]
    dres_ref, pay_ref = rest[4:6]
    wup, wdown, dd_s, ddt_s, nbt_s, dh_s, dnb_s, accd, accu, su, sd, sg, sb, sems = rest[6:]
    fetch_weights(section_ref, layer, own, other, (wup, wdown), sems)
    tokens, width = dy_ref.shape
    hidden_width = wup.shape[1]
    step = 64

    @pl.when(pl.program_id(0) == 0)
    def _():
        for ref in (accd, accu, su, sd, sg, sb):
            ref[...] = jnp.zeros_like(ref)

    gain_b, shift_b = vec1_ref[5:6, :], vec1_ref[6:7, :]
    for c in range(0, width, BLOCK):
        dd_s[:, c : c + BLOCK] = dy_ref[:, c : c + BLOCK] * valid_ref[...]
    ddt_s[...] = dd_s[...].T
    sd[...] += fold_rows(dd_s[...].astype(full))
    nbt_s[...] = (xhat_ref[...].astype(full) * gain_b + shift_b).astype(low).T
    for n0, n1 in column_blocks(hidden_width, 256):
        back = nt(dd_s[...], wdown[n0:n1, :])
        dh = (back * slope_ref[:, n0:n1].astype(full)).astype(low)
        dh_s[:, n0:n1] = dh
        su[:, n0:n1] += fold_rows(dh.astype(full))
        accd[:, n0:n1] += nn(ddt_s[...], act_ref[:, n0:n1])
        accu[:, n0:n1] += nn(nbt_s[...], dh)
    dnb_s[...] = nt(dh_s[...], wup[...])
    for t in range(0, tokens, step):
        scaled = xhat_ref[t : t + step, :].astype(full)
        inverse = inv_ref[t : t + step, :]
        inverse = jnp.concatenate([inverse] * (width // BLOCK), axis=1)
        dn = dnb_s[t : t + step, :]
        sg[...] += fold_rows(dn * scaled)
        sb[...] += fold_rows(dn)
        e = dn * gain_b
        inner = (e - jnp.mean(e, axis=-1, keepdims=True)) - scaled * jnp.mean(
            e * scaled, axis=-1, keepdims=True
        )
        dres_ref[t : t + step, :] = dd_s[t : t + step, :].astype(full) + inverse * inner

    @pl.when(pl.program_id(0) == pl.num_programs(0) - 1)
    def _():
        half = hidden_width // 2
        for h in range(2):
            for b in range(width // BLOCK):
                turned = accd[b * BLOCK : (b + 1) * BLOCK, h * half : (h + 1) * half].T
                pay_ref[h, b * half : (b + 1) * half, :] = turned.astype(low)
        base = half * (width // BLOCK)
        half = width // 2
        for h in range(2):
            for b in range(hidden_width // BLOCK):
                pay_ref[h, base + b * half : base + (b + 1) * half, :] = accu[
                    h * half : (h + 1) * half, b * BLOCK : (b + 1) * BLOCK
                ].astype(low)
        base += half * (hidden_width // BLOCK)
        store_small(pay_ref, base, [su[...], sd[...], sg[...], sb[...]])


def attention_backward_kernel(
    layer,
    slots,
    section_ref,
    x_ref,
    dres_ref,
    qkv_ref,
    e_ref,
    rinv_ref,
    mixed_ref,
    vec1_ref,
    *rest,
):
    own, other = rest[0:2], rest[2:4]
    dx_ref, pay_ref = rest[4:6]
    wqkv, wout, db_s, mixt_s, do_s, pr_s, dp_s, xh_s, iv_s, nat_s, dna_s = rest[6:17]
    accq, acco, sq, so, sg, sb, sems = rest[17:]
    fetch_weights(section_ref, layer, own, other, (wqkv, wout), sems)
    tokens, width = x_ref.shape
    step = 64

    @pl.when(pl.program_id(0) == 0)
    def _():
        for ref in (accq, acco, sq, so, sg, sb):
            ref[...] = jnp.zeros_like(ref)

    gain_a, shift_a = vec1_ref[0:1, :], vec1_ref[1:2, :]
    db_s[...] = dres_ref[...].astype(low)
    so[...] += fold_rows(db_s[...].astype(full))
    mixt_s[...] = mixed_ref[...].T
    acco[...] += nn(mixt_s[...], db_s[...])
    scaled_do = nt(db_s[...], wout[...]) * rinv_ref[...]
    do_s[...] = scaled_do.astype(low)
    pr_s[...] = (scaled_do * (-mixed_ref[...].astype(full))).astype(low)
    for t in range(0, tokens, step):
        scaled, inverse = norm_parts(x_ref[t : t + step, :].astype(full))
        xh_s[t : t + step, :] = scaled
        iv_s[t : t + step, :] = jnp.broadcast_to(inverse, (step, BLOCK))
        dna_s[t : t + step, :] = scaled * gain_a + shift_a
    nat_s[...] = dna_s[...].astype(low).T
    lanes = head_lanes()
    ones = jnp.ones((slots, BLOCK), low)
    for r in range(tokens // slots):
        rows = slice(r * slots, (r + 1) * slots)
        for p in range(H // 2):
            cols = slice(p * BLOCK, (p + 1) * BLOCK)
            q2 = qkv_ref[rows, p * BLOCK : (p + 1) * BLOCK]
            k2 = qkv_ref[rows, width + p * BLOCK : width + (p + 1) * BLOCK]
            v2 = qkv_ref[rows, 2 * width + p * BLOCK : 2 * width + (p + 1) * BLOCK]
            do2, pr2 = do_s[rows, cols], pr_s[rows, cols]
            values = jnp.concatenate([v2, ones], axis=1)
            weights, slopes, dos, qs, ks = [], [], [], [], []
            for i in range(2):
                e = e_ref[rows, (2 * p + i) * slots : (2 * p + i + 1) * slots]
                do = do2 * lanes[i]
                inner = nt(jnp.concatenate([do, pr2 * lanes[i]], axis=1), values)
                slopes.append((e.astype(full) * inner).astype(low))
                weights.append(e)
                dos.append(do)
                qs.append(q2 * lanes[i])
                ks.append(k2 * lanes[i])
            dv = tn(jnp.concatenate(weights, axis=0), jnp.concatenate(dos, axis=0))
            dk = tn(jnp.concatenate(slopes, axis=0), jnp.concatenate(qs, axis=0))
            dq = nn(jnp.concatenate(slopes, axis=1), jnp.concatenate(ks, axis=0)) * 0.125
            dp_s[rows, p * BLOCK : (p + 1) * BLOCK] = dq.astype(low)
            dp_s[rows, width + p * BLOCK : width + (p + 1) * BLOCK] = dk.astype(low)
            dp_s[rows, 2 * width + p * BLOCK : 2 * width + (p + 1) * BLOCK] = dv.astype(low)
    sq[:, :width] += fold_rows(dp_s[:, :width].astype(full))
    sq[:, width:] += fold_rows(dp_s[:, 2 * width :].astype(full))
    for n0, n1 in column_blocks(3 * width, 512):
        accq[:, n0:n1] += nn(nat_s[...], dp_s[:, n0:n1])
    dna_s[...] = nt(dp_s[...], wqkv[...])
    for t in range(0, tokens, step):
        scaled = xh_s[t : t + step, :]
        inverse = iv_s[t : t + step, :]
        inverse = jnp.concatenate([inverse] * (width // BLOCK), axis=1)
        dn = dna_s[t : t + step, :]
        sg[...] += fold_rows(dn * scaled)
        sb[...] += fold_rows(dn)
        e = dn * gain_a
        inner = (e - jnp.mean(e, axis=-1, keepdims=True)) - scaled * jnp.mean(
            e * scaled, axis=-1, keepdims=True
        )
        dx_ref[t : t + step, :] = (dres_ref[t : t + step, :] + inverse * inner).astype(low)

    @pl.when(pl.program_id(0) == pl.num_programs(0) - 1)
    def _():
        half = width // 2
        for h in range(2):
            for b in range(3 * width // BLOCK):
                pay_ref[h, b * half : (b + 1) * half, :] = accq[
                    h * half : (h + 1) * half, b * BLOCK : (b + 1) * BLOCK
                ].astype(low)
            base = half * (3 * width // BLOCK)
            for b in range(width // BLOCK):
                pay_ref[h, base + b * half : base + (b + 1) * half, :] = acco[
                    h * half : (h + 1) * half, b * BLOCK : (b + 1) * BLOCK
                ].astype(low)
        base = half * (4 * width // BLOCK)
        store_small(pay_ref, base, [sq[...], so[...], sg[...], sb[...]])


def call_kernel(kernel, section, steps, blocked, fixed, hbm, outs, fixed_outs, scratch, flops, moved):
    in_specs, args = [], []
    for array, shared in blocked:
        rows = array.shape[0] // (2 * steps if shared else steps)
        if shared:
            index = lambda i, s: (s[0] * steps + i, 0)
        else:
            index = lambda i, s: (i, 0)
        in_specs.append(pl.BlockSpec((rows, array.shape[1]), index))
        args.append(array)
    for array in fixed:
        in_specs.append(pl.BlockSpec(array.shape, lambda i, s, n=array.ndim: (0,) * n))
        args.append(array)
    for array in hbm:
        in_specs.append(pl.BlockSpec(memory_space=pl.ANY))
        args.append(array)
    out_specs, out_shapes = [], []
    for shape, dtype in outs:
        out_specs.append(pl.BlockSpec((shape[0] // steps, shape[1]), lambda i, s: (i, 0)))
        out_shapes.append(jax.ShapeDtypeStruct(shape, dtype))
    for shape, dtype in fixed_outs:
        out_specs.append(pl.BlockSpec(shape, lambda i, s, n=len(shape): (0,) * n))
        out_shapes.append(jax.ShapeDtypeStruct(shape, dtype))
    return pl.pallas_call(
        kernel,
        grid_spec=pltpu.PrefetchScalarGridSpec(
            num_scalar_prefetch=1,
            grid=(steps,),
            in_specs=in_specs,
            out_specs=out_specs,
            scratch_shapes=scratch,
        ),
        out_shape=out_shapes,
        compiler_params=pltpu.CompilerParams(vmem_limit_bytes=VMEM_LIMIT),
        cost_estimate=pl.CostEstimate(flops=flops, bytes_accessed=moved, transcendentals=0),
    )(section, *args)


def run_forward(layer, section, x, shared, masks, vec1, vecup, own, other, tokens, slots):
    width = x.shape[1]
    hidden_width = own[2].shape[1]
    steps = tokens // (R * slots)
    per_step = R * slots
    segment, block, valid = masks
    outs = [
        ((tokens, width), low),
        ((tokens, 3 * width), low),
        ((tokens, H * slots), low),
        ((tokens, width), full),
        ((tokens, width), low),
        ((tokens, width), low),
        ((tokens, BLOCK), full),
        ((tokens, hidden_width), low),
        ((tokens, hidden_width), low),
    ]
    scratch = [pltpu.VMEM(w.shape, low) for w in own] + [
        pltpu.VMEM((per_step, width), low),
        pltpu.VMEM((per_step, width), full),
        pltpu.VMEM((per_step, width), low),
        pltpu.SemaphoreType.DMA((4,)),
    ]
    return call_kernel(
        functools.partial(forward_kernel, layer, slots),
        section,
        steps,
        [(x, shared), (segment, True), (block, True), (valid, True)],
        [vec1, vecup],
        list(own) + list(other),
        outs,
        [],
        scratch,
        2 * tokens * (4 * width * width + 2 * width * hidden_width + 2 * slots * width),
        tokens * 14000,
    )


def run_ffn_backward(layer, section, dy, shared, valid, saved, vec1, own, other, tokens, slots):
    xhat, inv, act, slope = saved
    width, hidden_width = own[0].shape
    steps = tokens // (R * slots)
    per_step = R * slots
    pay_rows = hidden_width * width // BLOCK + SMALL_ROWS
    scratch = [
        pltpu.VMEM(own[0].shape, low),
        pltpu.VMEM(own[1].shape, low),
        pltpu.VMEM((per_step, width), low),
        pltpu.VMEM((width, per_step), low),
        pltpu.VMEM((width, per_step), low),
        pltpu.VMEM((per_step, hidden_width), low),
        pltpu.VMEM((per_step, width), full),
        pltpu.VMEM((width, hidden_width), full),
        pltpu.VMEM((width, hidden_width), full),
        pltpu.VMEM((8, hidden_width), full),
        pltpu.VMEM((8, width), full),
        pltpu.VMEM((8, width), full),
        pltpu.VMEM((8, width), full),
        pltpu.SemaphoreType.DMA((2,)),
    ]
    return call_kernel(
        functools.partial(ffn_backward_kernel, layer),
        section,
        steps,
        [(dy, shared), (valid, True), (xhat, False), (inv, False), (act, False), (slope, False)],
        [vec1],
        list(own) + list(other),
        [((tokens, width), full)],
        [((2, pay_rows, BLOCK), low)],
        scratch,
        8 * tokens * width * hidden_width,
        tokens * 10000,
    )


def run_attention_backward(layer, section, x, shared, saved, vec1, own, other, tokens, slots):
    dres, qkv, e, rinv, mixed = saved
    width = x.shape[1]
    steps = tokens // (R * slots)
    per_step = R * slots
    pay_rows = 2 * width * width // BLOCK + SMALL_ROWS
    scratch = [
        pltpu.VMEM(own[0].shape, low),
        pltpu.VMEM(own[1].shape, low),
        pltpu.VMEM((per_step, width), low),
        pltpu.VMEM((width, per_step), low),
        pltpu.VMEM((per_step, width), low),
        pltpu.VMEM((per_step, width), low),
        pltpu.VMEM((per_step, 3 * width), low),
        pltpu.VMEM((per_step, width), full),
        pltpu.VMEM((per_step, BLOCK), full),
        pltpu.VMEM((width, per_step), low),
        pltpu.VMEM((per_step, width), full),
        pltpu.VMEM((width, 3 * width), full),
        pltpu.VMEM((width, width), full),
        pltpu.VMEM((8, 2 * width), full),
        pltpu.VMEM((8, width), full),
        pltpu.VMEM((8, width), full),
        pltpu.VMEM((8, width), full),
        pltpu.SemaphoreType.DMA((2,)),
    ]
    return call_kernel(
        functools.partial(attention_backward_kernel, layer, slots),
        section,
        steps,
        [(x, shared), (dres, False), (qkv, False), (e, False), (rinv, False), (mixed, False)],
        [vec1],
        list(own) + list(other),
        [((tokens, width), low)],
        [((2, pay_rows, BLOCK), low)],
        scratch,
        2 * tokens * (8 * width * width + 5 * slots * width),
        tokens * 11000,
    )


SWAP = [(0, 1), (1, 0)]


def reduce_payload(pay, index):
    kept = lax.dynamic_index_in_dim(pay, index, 0, keepdims=False)
    sent = lax.dynamic_index_in_dim(pay, 1 - index, 0, keepdims=False)
    got = lax.ppermute(sent, "section", SWAP)
    return lax.psum(kept + got, "dp")


def merge_blocks(block, rows, columns):
    count = columns // BLOCK
    return block.reshape(count, rows, BLOCK).transpose(1, 0, 2).reshape(rows, columns)


def split_payload(first, second, shapes, small_sizes):
    result, base = [], 0
    for rows, columns in shapes:
        count = rows // 2 * columns // BLOCK
        parts = [
            merge_blocks(half[base : base + count], rows // 2, columns) for half in (first, second)
        ]
        result.append(jnp.concatenate(parts, axis=0).astype(full))
        base += count
    flat = first[base : base + sum(small_sizes) // BLOCK].reshape(-1).astype(full)
    start = 0
    for size in small_sizes:
        result.append(flat[start : start + size])
        start += size
    return result


def per_device(
    activations,
    cotangent,
    segment_ids,
    pad_mask,
    norm1_gain,
    norm1_bias,
    qkv_weight,
    qv_bias,
    out_weight,
    out_bias,
    norm2_gain,
    norm2_bias,
    up_weight,
    up_bias,
    down_weight,
    down_bias,
):
    index = lax.axis_index("section")
    section = index.astype(jnp.int32).reshape(1)
    is_first = index == 0
    local_rows, slots, width = activations.shape
    hidden_width = up_weight.shape[-1]
    tokens = local_rows // 2 * slots

    own = (qkv_weight[0], out_weight[0], up_weight[0], down_weight[0])
    vec1 = jnp.stack(
        [
            norm1_gain[0],
            norm1_bias[0],
            qv_bias[0, :width],
            qv_bias[0, width:],
            out_bias[0],
            norm2_gain[0],
            norm2_bias[0],
            down_bias[0],
        ]
    )
    vec = jnp.concatenate([vec1, up_bias.reshape(hidden_width // width, width)], axis=0)
    other_vec = lax.ppermute(vec, "section", SWAP)
    other = tuple(lax.ppermute(w, "section", SWAP) for w in own)
    vecs = []
    for layer in range(2):
        chosen = jnp.where(index == layer, vec, other_vec)
        vecs.append((chosen[:8], chosen[8:].reshape(1, hidden_width)))

    lane = lax.broadcasted_iota(jnp.int32, (1, 1, BLOCK), 2)
    segment = (segment_ids[:, :, None] == lane).astype(low).reshape(-1, BLOCK)
    open_keys = (segment_ids[:, :, None] == lane) & (pad_mask[:, :, None] > 0)
    block = jnp.where(open_keys, 0.0, forbidden).astype(low).reshape(-1, BLOCK)
    valid = jnp.broadcast_to(pad_mask[:, :, None].astype(low), (local_rows, slots, BLOCK))
    valid = valid.reshape(-1, BLOCK)
    masks = (segment, block, valid)
    x = activations.reshape(-1, width)
    seed = cotangent.reshape(-1, width)

    saved = []
    inputs, shared = x, True
    outs = []
    for layer in range(2):
        out, *kept = run_forward(
            layer, section, inputs, shared, masks, *vecs[layer], own, other, tokens, slots
        )
        saved.append((inputs, shared, kept))
        outs.append(out)
        inputs, shared = out, False

    dy, dy_shared = seed, True
    grads = [None, None]
    reduced = [None, None]
    for layer in (1, 0):
        layer_x, x_shared, (qkv, e, rinv, mixed, xhat, inv, act, slope) = saved[layer]
        dres, ffn_pay = run_ffn_backward(
            layer,
            section,
            dy,
            dy_shared,
            valid,
            (xhat, inv, act, slope),
            vecs[layer][0],
            own[2:],
            other[2:],
            tokens,
            slots,
        )
        ffn_sum = reduce_payload(ffn_pay, index)
        dx, attn_pay = run_attention_backward(
            layer,
            section,
            layer_x,
            x_shared,
            (dres, qkv, e, rinv, mixed),
            vecs[layer][0],
            own[:2],
            other[:2],
            tokens,
            slots,
        )
        attn_sum = reduce_payload(attn_pay, index)
        grads[layer] = dx
        reduced[layer] = (ffn_sum, attn_sum)
        dy, dy_shared = dx, False

    to_second, to_first = [(0, 1)], [(1, 0)]

    def assemble(pair, dtype):
        from_second = lax.ppermute(pair[0], "section", to_first)
        from_first = lax.ppermute(pair[1], "section", to_second)
        top = jnp.where(is_first, pair[0], from_first)
        bottom = jnp.where(is_first, from_second, pair[1])
        joined = jnp.concatenate([top, bottom], axis=0).astype(dtype)
        return joined.reshape(1, local_rows, slots, width)

    def join_sums(first_layer, second_layer):
        from_second = lax.ppermute(first_layer, "section", to_first)
        from_first = lax.ppermute(second_layer, "section", to_second)
        return (
            jnp.where(is_first, first_layer, from_first),
            jnp.where(is_first, from_second, second_layer),
        )

    layer_outs = assemble(outs, low)
    layer_in_grads = assemble(grads, full)
    down_grad, up_grad, up_b, down_b, gain2, shift2 = split_payload(
        *join_sums(reduced[0][0], reduced[1][0]),
        [(hidden_width, width), (width, hidden_width)],
        [hidden_width, width, width, width],
    )
    qkv_grad, out_grad, qv_b, out_b, gain1, shift1 = split_payload(
        *join_sums(reduced[0][1], reduced[1][1]),
        [(width, 3 * width), (width, width)],
        [2 * width, width, width, width],
    )
    ordered = (
        gain1,
        shift1,
        qkv_grad,
        qv_b,
        out_grad,
        out_b,
        gain2,
        shift2,
        up_grad,
        up_b,
        down_grad,
        down_b,
    )
    return (layer_outs, layer_in_grads) + tuple(value[None] for value in ordered)


def solution(mesh):
    in_specs = (
        P("dp", None, None),
        P("dp", None, None),
        P("dp", None),
        P("dp", None),
        P("section", None),
        P("section", None),
        P("section", None, None),
        P("section", None),
        P("section", None, None),
        P("section", None),
        P("section", None),
        P("section", None),
        P("section", None, None),
        P("section", None),
        P("section", None, None),
        P("section", None),
    )
    out_specs = (
        P("section", "dp", None, None),
        P("section", "dp", None, None),
        P("section", None),
        P("section", None),
        P("section", None, None),
        P("section", None),
        P("section", None, None),
        P("section", None),
        P("section", None),
        P("section", None),
        P("section", None, None),
        P("section", None),
        P("section", None, None),
        P("section", None),
    )
    return jax.shard_map(
        per_device, mesh=mesh, in_specs=in_specs, out_specs=out_specs, check_vma=False
    )
```

```python
import functools

import jax
import jax.numpy as jnp
from jax import lax
from jax.experimental import pallas as pl
from jax.experimental.pallas import tpu as pltpu
from jax.sharding import PartitionSpec as P

H = 6
R_F, R_FB, R_AB = 1, 2, 2
BLOCK = 128
norm_eps = 1e-06
forbidden = -1e30
sqrt_half = 0.7071067811865476
inverse_root_two_pi = 0.3989422804014327
VMEM_LIMIT = 60 * 1024 * 1024
low = jnp.bfloat16
full = jnp.float32


def nn(a, b):
    return lax.dot_general(a, b, (((1,), (0,)), ((), ())), preferred_element_type=full)


def nt(a, b):
    return lax.dot_general(a, b, (((1,), (1,)), ((), ())), preferred_element_type=full)


def tn(a, b):
    return lax.dot_general(a, b, (((0,), (0,)), ((), ())), preferred_element_type=full)


def column_blocks(width, step):
    return [(start, min(start + step, width)) for start in range(0, width, step)]


def fold_rows(values):
    return jnp.sum(values.reshape(values.shape[0] // 8, 8, values.shape[1]), axis=0)


def gelu_parts(hidden):
    size = jnp.abs(hidden)
    t = pl.reciprocal(1.0 + (0.3275911 * sqrt_half) * size, approx=True)
    bell = jnp.exp(-0.5 * (hidden * hidden))
    series = t * (
        0.127414796
        + t * (-0.142248368 + t * (0.7107068705 + t * (-0.7265760135 + t * 0.5307027145)))
    )
    tail = series * bell
    cdf = jnp.where(hidden >= 0.0, 1.0 - tail, tail)
    return (hidden * cdf, cdf + (hidden * inverse_root_two_pi) * bell)


def norm_parts(values):
    average = jnp.mean(values, axis=-1, keepdims=True)
    centred = values - average
    inverse = lax.rsqrt(jnp.mean(centred * centred, axis=-1, keepdims=True) + norm_eps)
    return (centred * inverse, inverse)


def head_lanes():
    lane = lax.broadcasted_iota(jnp.int32, (1, BLOCK), 1)
    first = jnp.where(lane < BLOCK // 2, 1.0, 0.0)
    return (first.astype(low), (1.0 - first).astype(low))


def fetch_weights(scal_ref, layer, own, other, held, sems):
    @pl.when(pl.program_id(0) == 0)
    def _():
        @pl.when(scal_ref[0] == layer)
        def _():
            for i in range(len(own)):
                pltpu.make_async_copy(own[i], held[i], sems.at[i]).start()

        @pl.when(scal_ref[0] != layer)
        def _():
            for i in range(len(own)):
                pltpu.make_async_copy(other[i], held[i], sems.at[i]).start()

        for i in range(len(own)):
            pltpu.make_async_copy(own[i], held[i], sems.at[i]).wait()


def row_index(scal_ref, steps_rows, r):
    return (scal_ref[0] * pl.num_programs(0) + pl.program_id(0)) * steps_rows + r


def pack_kernel(g1, b1, qv, ob, g2, b2, ub, db, out_ref):
    width = g1.shape[1]
    rows = [g1[...], b1[...], qv[:, :width], qv[:, width:], ob[...], g2[...], b2[...], db[...]]
    rows += [ub[:, c : c + width] for c in range(0, ub.shape[1], width)]
    out_ref[...] = jnp.concatenate(rows, axis=0)


def forward_kernel(layer, slots, scal_ref, x_ref, seg_ref, pad_ref, *rest):
    own, other = rest[0:5], rest[5:10]
    rest = rest[10:]
    if layer == 0:
        out_ref, rest = rest[0], rest[1:]
    else:
        send_ref, mine_ref, rest = rest[0], rest[1], rest[2:]
    qkv_ref, e_ref, rinv_ref, mixed_ref, xhat_ref, inv_ref, act_ref, slope_ref = rest[:8]
    wqkv, wout, wup, wdown, vec, na_s, res_s, nb_s, sg_s, bk_s, va_s, sems = rest[8:]
    fetch_weights(scal_ref, layer, own, other, (wqkv, wout, wup, wdown, vec), sems)
    tokens, width = x_ref.shape
    hidden_width = wup.shape[1]
    step = 64
    gain_a, shift_a = vec[0:1, :], vec[1:2, :]
    q_off, v_off = vec[2:3, :], vec[3:4, :]
    out_off, gain_b, shift_b, down_off = (vec[i : i + 1, :] for i in range(4, 8))
    for t in range(0, tokens, step):
        scaled, _ = norm_parts(x_ref[t : t + step, :].astype(full))
        na_s[t : t + step, :] = (scaled * gain_a + shift_a).astype(low)
    code = lax.broadcasted_iota(jnp.int32, (BLOCK, slots), 0)
    for r in range(tokens // slots):
        rows = slice(r * slots, (r + 1) * slots)
        row = row_index(scal_ref, tokens // slots, r)
        same = seg_ref[pl.ds(row, 1), :] == code
        pad = pad_ref[pl.ds(row, 1), :]
        sg_s[rows, :] = jnp.where(same, 1.0, 0.0).T.astype(low)
        bk_s[rows, :] = jnp.where(same & (pad > 0), 0.0, forbidden).T.astype(low)
        va_s[rows, :] = jnp.broadcast_to(pad.astype(full), (BLOCK, slots)).T
    for n0, n1 in column_blocks(3 * width, 512):
        part = nn(na_s[...], wqkv[:, n0:n1])
        for c in range(n0, n1, BLOCK):
            piece = part[:, c - n0 : c - n0 + BLOCK]
            if c < width:
                piece = (piece + q_off[:, c : c + BLOCK]) * 0.125
            elif c >= 2 * width:
                piece = piece + v_off[:, c - 2 * width : c - 2 * width + BLOCK]
            qkv_ref[:, c : c + BLOCK] = piece.astype(low)
    lanes = head_lanes()
    ones = jnp.ones((slots, BLOCK), low)
    for r in range(tokens // slots):
        rows = slice(r * slots, (r + 1) * slots)
        for p in range(H // 2):
            q2 = qkv_ref[rows, p * BLOCK : (p + 1) * BLOCK]
            k2 = qkv_ref[rows, width + p * BLOCK : width + (p + 1) * BLOCK]
            v2 = qkv_ref[rows, 2 * width + p * BLOCK : 2 * width + (p + 1) * BLOCK]
            keys = jnp.concatenate([k2, bk_s[rows, :]], axis=1)
            weights = []
            for i in range(2):
                queries = jnp.concatenate([q2 * lanes[i], sg_s[rows, :]], axis=1)
                scores = nt(queries, keys)
                e = jnp.exp(scores - jnp.max(scores, axis=1, keepdims=True)).astype(low)
                e_ref[rows, (2 * p + i) * slots : (2 * p + i + 1) * slots] = e
                weights.append(e)
            values = jnp.concatenate(
                [
                    jnp.concatenate([v2 * lanes[0], ones * lanes[0]], axis=1),
                    jnp.concatenate([v2 * lanes[1], ones * lanes[1]], axis=1),
                ],
                axis=0,
            )
            both = nn(jnp.concatenate(weights, axis=1), values)
            rinv = 1.0 / both[:, BLOCK:]
            rinv_ref[rows, p * BLOCK : (p + 1) * BLOCK] = rinv
            mixed_ref[rows, p * BLOCK : (p + 1) * BLOCK] = (both[:, :BLOCK] * rinv).astype(low)
    res_s[...] = x_ref[...].astype(full) + (nn(mixed_ref[...], wout[...]) + out_off)
    for t in range(0, tokens, step):
        scaled, inverse = norm_parts(res_s[t : t + step, :])
        xhat_ref[t : t + step, :] = scaled.astype(low)
        inv_ref[t : t + step, :] = jnp.broadcast_to(inverse, (step, BLOCK))
        nb_s[t : t + step, :] = (scaled * gain_b + shift_b).astype(low)
    for n0, n1 in column_blocks(hidden_width, 256):
        offset = jnp.concatenate(
            [
                vec[8 + c // width : 9 + c // width, c % width : c % width + BLOCK]
                for c in range(n0, n1, BLOCK)
            ],
            axis=1,
        )
        act, slope = gelu_parts(nn(nb_s[...], wup[:, n0:n1]) + offset)
        act_ref[:, n0:n1] = act.astype(low)
        slope_ref[:, n0:n1] = slope.astype(low)
    outcome = res_s[...] + (nn(act_ref[...], wdown[...]) + down_off)
    for c in range(0, width, BLOCK):
        piece = (va_s[...] * outcome[:, c : c + BLOCK]).astype(low)
        if layer == 0:
            out_ref[:, c : c + BLOCK] = piece
        else:
            before = x_ref[:, c : c + BLOCK]

            @pl.when(scal_ref[0] == 0)
            def _():
                send_ref[:, c : c + BLOCK] = piece
                mine_ref[:, c : c + BLOCK] = before

            @pl.when(scal_ref[0] != 0)
            def _():
                send_ref[:, c : c + BLOCK] = before
                mine_ref[:, c : c + BLOCK] = piece


def small_block(vectors):
    row = jnp.concatenate([jnp.sum(v, axis=0, keepdims=True) for v in vectors], axis=1)
    count = row.shape[1] // BLOCK
    pieces = [row[:, j * BLOCK : (j + 1) * BLOCK] for j in range(count)]
    padded = -(-count // 16) * 16
    if padded > count:
        pieces.append(jnp.zeros((padded - count, BLOCK), full))
    return jnp.concatenate(pieces, axis=0).astype(low)


def store_payload(scal_ref, keep_ref, send_ref, write):
    for h in range(2):

        @pl.when(scal_ref[0] == h)
        def _():
            write(keep_ref, h)

        @pl.when(scal_ref[0] != h)
        def _():
            write(send_ref, h)


def store_columns(ref, base, matrix, row0, rows):
    for b in range(matrix.shape[1] // BLOCK):
        ref[base + b * rows : base + (b + 1) * rows, :] = matrix[
            row0 : row0 + rows, b * BLOCK : (b + 1) * BLOCK
        ].astype(low)
    return base + rows * (matrix.shape[1] // BLOCK)


def store_rest(ref, base, block):
    ref[base : base + block.shape[0], :] = block
    base += block.shape[0]
    if base < ref.shape[0]:
        ref[base:, :] = jnp.zeros((ref.shape[0] - base, BLOCK), low)


def ffn_backward_kernel(
    layer, slots, scal_ref, dy_ref, xhat_ref, inv_ref, act_ref, slope_ref, pad_ref, *rest
):
    own, other = rest[0:3], rest[3:6]
    dres_ref, keep_ref, send_ref = rest[6:9]
    wup, wdown, vec, dd_s, ddt_s, nbt_s, dh_s, dnb_s, accd, accu, su, sd, sg, sb, sems = rest[9:]
    fetch_weights(scal_ref, layer, own, other, (wup, wdown, vec), sems)
    tokens, width = dy_ref.shape
    hidden_width = wup.shape[1]
    step = 64

    @pl.when(pl.program_id(0) == 0)
    def _():
        for ref in (accd, accu, su, sd, sg, sb):
            ref[...] = jnp.zeros_like(ref)

    gain_b, shift_b = vec[5:6, :], vec[6:7, :]
    for r in range(tokens // slots):
        rows = slice(r * slots, (r + 1) * slots)
        row = row_index(scal_ref, tokens // slots, r)
        pad = pad_ref[pl.ds(row, 1), :].astype(full)
        valid = jnp.broadcast_to(pad, (BLOCK, slots)).T.astype(low)
        for c in range(0, width, BLOCK):
            dd_s[rows, c : c + BLOCK] = dy_ref[rows, c : c + BLOCK] * valid
    ddt_s[...] = dd_s[...].T
    sd[...] += fold_rows(dd_s[...].astype(full))
    nbt_s[...] = (xhat_ref[...].astype(full) * gain_b + shift_b).astype(low).T
    for n0, n1 in column_blocks(hidden_width, 256):
        back = nt(dd_s[...], wdown[n0:n1, :])
        dh = (back * slope_ref[:, n0:n1].astype(full)).astype(low)
        dh_s[:, n0:n1] = dh
        su[:, n0:n1] += fold_rows(dh.astype(full))
        accd[:, n0:n1] += nn(ddt_s[...], act_ref[:, n0:n1])
        accu[:, n0:n1] += nn(nbt_s[...], dh)
    dnb_s[...] = nt(dh_s[...], wup[...])
    for t in range(0, tokens, step):
        scaled = xhat_ref[t : t + step, :].astype(full)
        inverse = inv_ref[t : t + step, :]
        inverse = jnp.concatenate([inverse] * (width // BLOCK), axis=1)
        dn = dnb_s[t : t + step, :]
        sg[...] += fold_rows(dn * scaled)
        sb[...] += fold_rows(dn)
        e = dn * gain_b
        inner = (e - jnp.mean(e, axis=-1, keepdims=True)) - scaled * jnp.mean(
            e * scaled, axis=-1, keepdims=True
        )
        dres_ref[t : t + step, :] = dd_s[t : t + step, :].astype(full) + inverse * inner

    @pl.when(pl.program_id(0) == pl.num_programs(0) - 1)
    def _():
        small = small_block([su[...], sd[...], sg[...], sb[...]])

        def write(ref, h):
            half = hidden_width // 2
            for b in range(width // BLOCK):
                turned = accd[b * BLOCK : (b + 1) * BLOCK, h * half : (h + 1) * half].T
                ref[b * half : (b + 1) * half, :] = turned.astype(low)
            base = store_columns(ref, half * (width // BLOCK), accu, h * width // 2, width // 2)
            store_rest(ref, base, small)

        store_payload(scal_ref, keep_ref, send_ref, write)


def attention_backward_kernel(
    layer, slots, scal_ref, x_ref, dres_ref, qkv_ref, e_ref, rinv_ref, mixed_ref, *rest
):
    if layer == 0:
        later_ref, rest = rest[0], rest[1:]
    own, other, rest = rest[0:3], rest[3:6], rest[6:]
    if layer == 0:
        dsend_ref, dmine_ref, rest = rest[0], rest[1], rest[2:]
    else:
        dx_ref, rest = rest[0], rest[1:]
    keep_ref, send_ref = rest[0:2]
    wqkv, wout, vec, db_s, mixt_s, do_s, pr_s, dp_s, xh_s, iv_s, nat_s, dna_s = rest[2:14]
    accq, acco, sq, so, sg, sb, sems = rest[14:]
    fetch_weights(scal_ref, layer, own, other, (wqkv, wout, vec), sems)
    tokens, width = x_ref.shape
    step = 64

    @pl.when(pl.program_id(0) == 0)
    def _():
        for ref in (accq, acco, sq, so, sg, sb):
            ref[...] = jnp.zeros_like(ref)

    gain_a, shift_a = vec[0:1, :], vec[1:2, :]
    db_s[...] = dres_ref[...].astype(low)
    so[...] += fold_rows(db_s[...].astype(full))
    mixt_s[...] = mixed_ref[...].T
    acco[...] += nn(mixt_s[...], db_s[...])
    scaled_do = nt(db_s[...], wout[...]) * rinv_ref[...]
    do_s[...] = scaled_do.astype(low)
    pr_s[...] = (scaled_do * (-mixed_ref[...].astype(full))).astype(low)
    for t in range(0, tokens, step):
        scaled, inverse = norm_parts(x_ref[t : t + step, :].astype(full))
        xh_s[t : t + step, :] = scaled
        iv_s[t : t + step, :] = jnp.broadcast_to(inverse, (step, BLOCK))
        dna_s[t : t + step, :] = scaled * gain_a + shift_a
    nat_s[...] = dna_s[...].astype(low).T
    lanes = head_lanes()
    ones = jnp.ones((slots, BLOCK), low)
    for r in range(tokens // slots):
        rows = slice(r * slots, (r + 1) * slots)
        for p in range(H // 2):
            cols = slice(p * BLOCK, (p + 1) * BLOCK)
            q2 = qkv_ref[rows, p * BLOCK : (p + 1) * BLOCK]
            k2 = qkv_ref[rows, width + p * BLOCK : width + (p + 1) * BLOCK]
            v2 = qkv_ref[rows, 2 * width + p * BLOCK : 2 * width + (p + 1) * BLOCK]
            do2, pr2 = do_s[rows, cols], pr_s[rows, cols]
            values = jnp.concatenate([v2, ones], axis=1)
            weights, slopes, dos, qs, ks = [], [], [], [], []
            for i in range(2):
                e = e_ref[rows, (2 * p + i) * slots : (2 * p + i + 1) * slots]
                do = do2 * lanes[i]
                inner = nt(jnp.concatenate([do, pr2 * lanes[i]], axis=1), values)
                slopes.append((e.astype(full) * inner).astype(low))
                weights.append(e)
                dos.append(do)
                qs.append(q2 * lanes[i])
                ks.append(k2 * lanes[i])
            dv = tn(jnp.concatenate(weights, axis=0), jnp.concatenate(dos, axis=0))
            dk = tn(jnp.concatenate(slopes, axis=0), jnp.concatenate(qs, axis=0))
            dq = nn(jnp.concatenate(slopes, axis=1), jnp.concatenate(ks, axis=0)) * 0.125
            dp_s[rows, p * BLOCK : (p + 1) * BLOCK] = dq.astype(low)
            dp_s[rows, width + p * BLOCK : width + (p + 1) * BLOCK] = dk.astype(low)
            dp_s[rows, 2 * width + p * BLOCK : 2 * width + (p + 1) * BLOCK] = dv.astype(low)
    sq[:, :width] += fold_rows(dp_s[:, :width].astype(full))
    sq[:, width:] += fold_rows(dp_s[:, 2 * width :].astype(full))
    for n0, n1 in column_blocks(3 * width, 512):
        accq[:, n0:n1] += nn(nat_s[...], dp_s[:, n0:n1])
    dna_s[...] = nt(dp_s[...], wqkv[...])
    for t in range(0, tokens, step):
        part = slice(t, t + step)
        scaled = xh_s[part, :]
        inverse = iv_s[part, :]
        inverse = jnp.concatenate([inverse] * (width // BLOCK), axis=1)
        dn = dna_s[part, :]
        sg[...] += fold_rows(dn * scaled)
        sb[...] += fold_rows(dn)
        e = dn * gain_a
        inner = (e - jnp.mean(e, axis=-1, keepdims=True)) - scaled * jnp.mean(
            e * scaled, axis=-1, keepdims=True
        )
        dna_s[part, :] = dres_ref[part, :] + inverse * inner
    if layer == 0:

        @pl.when(scal_ref[0] == 0)
        def _():
            dmine_ref[...] = dna_s[...]
            dsend_ref[...] = later_ref[...]

        @pl.when(scal_ref[0] != 0)
        def _():
            dmine_ref[...] = later_ref[...].astype(full)
            dsend_ref[...] = dna_s[...].astype(low)

    else:
        dx_ref[...] = dna_s[...].astype(low)

    @pl.when(pl.program_id(0) == pl.num_programs(0) - 1)
    def _():
        small = small_block([sq[...], so[...], sg[...], sb[...]])

        def write(ref, h):
            base = store_columns(ref, 0, accq, h * width // 2, width // 2)
            base = store_columns(ref, base, acco, h * width // 2, width // 2)
            store_rest(ref, base, small)

        store_payload(scal_ref, keep_ref, send_ref, write)


def call_kernel(kernel, scal, steps, blocked, fixed, hbm, outs, fixed_outs, scratch, flops, moved):
    own_index = lambda i, s: (i, 0)
    shared_index = lambda i, s: (s[0] * steps + i, 0)

    def spec(shape, shared):
        rows = shape[0] // (2 * steps if shared else steps)
        return pl.BlockSpec((rows, shape[1]), shared_index if shared else own_index)

    in_specs, args = [], []
    for array, shared in blocked:
        in_specs.append(spec(array.shape, shared))
        args.append(array)
    for array in fixed:
        in_specs.append(pl.BlockSpec(array.shape, lambda i, s, n=array.ndim: (0,) * n))
        args.append(array)
    for array in hbm:
        in_specs.append(pl.BlockSpec(memory_space=pl.ANY))
        args.append(array)
    out_specs, out_shapes = [], []
    for shape, dtype, shared in outs:
        out_specs.append(spec(shape, shared))
        out_shapes.append(jax.ShapeDtypeStruct(shape, dtype))
    for shape, dtype in fixed_outs:
        out_specs.append(pl.BlockSpec(shape, lambda i, s, n=len(shape): (0,) * n))
        out_shapes.append(jax.ShapeDtypeStruct(shape, dtype))
    return pl.pallas_call(
        kernel,
        grid_spec=pltpu.PrefetchScalarGridSpec(
            num_scalar_prefetch=1,
            grid=(steps,),
            in_specs=in_specs,
            out_specs=out_specs,
            scratch_shapes=scratch,
        ),
        out_shape=out_shapes,
        compiler_params=pltpu.CompilerParams(vmem_limit_bytes=VMEM_LIMIT),
        cost_estimate=pl.CostEstimate(flops=flops, bytes_accessed=moved, transcendentals=0),
    )(scal, *args)


def run_forward(layer, scal, x, shared, segments, pad, own, other, tokens, slots):
    width = x.shape[1]
    hidden_width = own[2].shape[1]
    steps = tokens // (R_F * slots)
    per_step = R_F * slots
    if layer == 0:
        outs = [((tokens, width), low, False)]
    else:
        outs = [((tokens, width), low, False), ((2 * tokens, width), low, True)]
    outs += [
        ((tokens, 3 * width), low, False),
        ((tokens, H * slots), low, False),
        ((tokens, width), full, False),
        ((tokens, width), low, False),
        ((tokens, width), low, False),
        ((tokens, BLOCK), full, False),
        ((tokens, hidden_width), low, False),
        ((tokens, hidden_width), low, False),
    ]
    scratch = [pltpu.VMEM(w.shape, w.dtype) for w in own] + [
        pltpu.VMEM((per_step, width), low),
        pltpu.VMEM((per_step, width), full),
        pltpu.VMEM((per_step, width), low),
        pltpu.VMEM((per_step, BLOCK), low),
        pltpu.VMEM((per_step, BLOCK), low),
        pltpu.VMEM((per_step, BLOCK), full),
        pltpu.SemaphoreType.DMA((5,)),
    ]
    return call_kernel(
        functools.partial(forward_kernel, layer, slots),
        scal,
        steps,
        [(x, shared)],
        [segments, pad],
        list(own) + list(other),
        outs,
        [],
        scratch,
        2 * tokens * (4 * width * width + 2 * width * hidden_width + 2 * slots * width),
        tokens * 14000,
    )


def payload_rows(used, devices):
    unit = devices * 16
    return -(-used // unit) * unit


def run_ffn_backward(layer, scal, dy, shared, pad, saved, own, other, tokens, slots, devices):
    width, hidden_width = own[0].shape
    steps = tokens // (R_FB * slots)
    per_step = R_FB * slots
    rows = payload_rows(hidden_width * width // BLOCK + 32, devices)
    scratch = [pltpu.VMEM(w.shape, w.dtype) for w in own] + [
        pltpu.VMEM((per_step, width), low),
        pltpu.VMEM((width, per_step), low),
        pltpu.VMEM((width, per_step), low),
        pltpu.VMEM((per_step, hidden_width), low),
        pltpu.VMEM((per_step, width), full),
        pltpu.VMEM((width, hidden_width), full),
        pltpu.VMEM((width, hidden_width), full),
        pltpu.VMEM((8, hidden_width), full),
        pltpu.VMEM((8, width), full),
        pltpu.VMEM((8, width), full),
        pltpu.VMEM((8, width), full),
        pltpu.SemaphoreType.DMA((3,)),
    ]
    return call_kernel(
        functools.partial(ffn_backward_kernel, layer, slots),
        scal,
        steps,
        [(dy, shared)] + [(array, False) for array in saved],
        [pad],
        list(own) + list(other),
        [((tokens, width), full, False)],
        [((rows, BLOCK), low), ((rows, BLOCK), low)],
        scratch,
        8 * tokens * width * hidden_width,
        tokens * 10000,
    )


def run_attention_backward(layer, scal, x, shared, saved, later, own, other, tokens, slots, devices):
    width = x.shape[1]
    steps = tokens // (R_AB * slots)
    per_step = R_AB * slots
    rows = payload_rows(2 * width * width // BLOCK + 16, devices)
    blocked = [(x, shared)] + [(array, False) for array in saved]
    if layer == 0:
        blocked.append((later, False))
        outs = [((tokens, width), low, False), ((2 * tokens, width), full, True)]
    else:
        outs = [((tokens, width), low, False)]
    scratch = [pltpu.VMEM(w.shape, w.dtype) for w in own] + [
        pltpu.VMEM((per_step, width), low),
        pltpu.VMEM((width, per_step), low),
        pltpu.VMEM((per_step, width), low),
        pltpu.VMEM((per_step, width), low),
        pltpu.VMEM((per_step, 3 * width), low),
        pltpu.VMEM((per_step, width), full),
        pltpu.VMEM((per_step, BLOCK), full),
        pltpu.VMEM((width, per_step), low),
        pltpu.VMEM((per_step, width), full),
        pltpu.VMEM((width, 3 * width), full),
        pltpu.VMEM((width, width), full),
        pltpu.VMEM((8, 2 * width), full),
        pltpu.VMEM((8, width), full),
        pltpu.VMEM((8, width), full),
        pltpu.VMEM((8, width), full),
        pltpu.SemaphoreType.DMA((3,)),
    ]
    return call_kernel(
        functools.partial(attention_backward_kernel, layer, slots),
        scal,
        steps,
        blocked,
        [],
        list(own) + list(other),
        outs,
        [((rows, BLOCK), low), ((rows, BLOCK), low)],
        scratch,
        2 * tokens * (8 * width * width + 5 * slots * width),
        tokens * 11000,
    )


def fill_kernel(scal_ref, got_ref, held_ref, out_ref):
    del scal_ref, held_ref
    out_ref[...] = got_ref[...].astype(out_ref.dtype)


def fill_other_half(scal, held, got, steps):
    rows = got.shape[0] // steps
    return pl.pallas_call(
        fill_kernel,
        grid_spec=pltpu.PrefetchScalarGridSpec(
            num_scalar_prefetch=1,
            grid=(steps,),
            in_specs=[
                pl.BlockSpec((rows, got.shape[1]), lambda i, s: (i, 0)),
                pl.BlockSpec(memory_space=pl.ANY),
            ],
            out_specs=pl.BlockSpec(
                (rows, got.shape[1]), lambda i, s: ((1 - s[0]) * steps + i, 0)
            ),
        ),
        out_shape=jax.ShapeDtypeStruct(held.shape, held.dtype),
        input_output_aliases={2: 0},
        cost_estimate=pl.CostEstimate(
            flops=0, bytes_accessed=8 * got.size, transcendentals=0
        ),
    )(scal, got, held)


def sum_kernel(count, size, scal_ref, *refs):
    del scal_ref
    for j in range(size):
        total = refs[j * count][...].astype(full)
        for a in range(1, count):
            total = total + refs[j * count + a][...].astype(full)
        refs[size * count + j][...] = total.astype(low)


def scatter_sums(scal, arrays, place, size):
    rows = arrays[0].shape[0] // size
    in_specs, args = [], []
    for j in range(size):
        for array in arrays:
            if size == 1:
                index = lambda i, s: (0, 0)
            else:
                index = lambda i, s, j=j: (s[place] ^ j, 0)
            in_specs.append(pl.BlockSpec((rows, BLOCK), index))
            args.append(array)
    return pl.pallas_call(
        functools.partial(sum_kernel, len(arrays), size),
        grid_spec=pltpu.PrefetchScalarGridSpec(
            num_scalar_prefetch=1,
            grid=(1,),
            in_specs=in_specs,
            out_specs=[pl.BlockSpec((rows, BLOCK), lambda i, s: (0, 0))] * size,
        ),
        out_shape=[jax.ShapeDtypeStruct((rows, BLOCK), low)] * size,
        compiler_params=pltpu.CompilerParams(vmem_limit_bytes=VMEM_LIMIT),
        cost_estimate=pl.CostEstimate(
            flops=0, bytes_accessed=4 * arrays[0].size * len(arrays), transcendentals=0
        ),
    )(scal, *args)


def place_pieces(scal_ref, place, pieces, out_ref):
    rows = pieces[0].shape[0]
    for j, piece in enumerate(pieces):
        start = pl.multiple_of((scal_ref[place] ^ j) * rows, 16)
        out_ref[pl.ds(start, rows), :] = piece[...]


def gather_kernel(place, scal_ref, *refs):
    place_pieces(scal_ref, place, refs[:-1], refs[-1])


def single_step(kernel, scal, arrays, shapes, scratch=()):
    whole = lambda shape: pl.BlockSpec(shape, lambda i, s, n=len(shape): (0,) * n)
    moved = sum(a.size * a.dtype.itemsize for a in arrays)
    return pl.pallas_call(
        kernel,
        grid_spec=pltpu.PrefetchScalarGridSpec(
            num_scalar_prefetch=1,
            grid=(1,),
            in_specs=[whole(a.shape) for a in arrays],
            out_specs=[whole(shape) for shape, _ in shapes],
            scratch_shapes=list(scratch),
        ),
        out_shape=[jax.ShapeDtypeStruct(shape, dtype) for shape, dtype in shapes],
        compiler_params=pltpu.CompilerParams(vmem_limit_bytes=VMEM_LIMIT),
        cost_estimate=pl.CostEstimate(flops=0, bytes_accessed=3 * moved, transcendentals=0),
    )(scal, *arrays)


def choose_kernel(place, scal_ref, *refs):
    out_ref = refs[-1]

    @pl.when(scal_ref[0] == 0)
    def _():
        out_ref[...] = refs[-2][...]

    @pl.when(scal_ref[0] != 0)
    def _():
        place_pieces(scal_ref, place, refs[:-2], out_ref)


def unpack_kernel(place, count, shapes, smalls, scal_ref, *refs):
    pieces, second, got = refs[:count], refs[count], refs[count + 1]
    matrices = refs[count + 2 : count + 2 + len(shapes)]
    vectors, mine = refs[count + 2 + len(shapes) : -1], refs[-1]

    @pl.when(scal_ref[0] == 0)
    def _():
        place_pieces(scal_ref, place, pieces, mine)

    @pl.when(scal_ref[0] != 0)
    def _():
        mine[...] = second[...]

    def write(source, h):
        base = 0
        for (rows, columns), out_ref in zip(shapes, matrices):
            half = rows // 2
            for b in range(columns // BLOCK):
                out_ref[0, h * half : (h + 1) * half, b * BLOCK : (b + 1) * BLOCK] = source[
                    base : base + half, :
                ].astype(full)
                base += half
        return base

    for h in range(2):

        @pl.when(scal_ref[0] == h)
        def _():
            write(mine, h)

        @pl.when(scal_ref[0] != h)
        def _():
            write(got, h)

    base = sum(rows // 2 * columns // BLOCK for rows, columns in shapes)
    padded = -(-sum(smalls) // BLOCK // 16) * 16
    block = mine[base : base + padded, :].astype(full)
    row = 0
    for size, out_ref in zip(smalls, vectors):
        for c in range(0, size, BLOCK):
            out_ref[0:1, c : c + BLOCK] = block[row : row + 1, :]
            row += 1


SWAP = [(0, 1), (1, 0)]


def stage_sizes(devices):
    sizes = []
    while devices > 1:
        size = 4 if devices % 4 == 0 and devices != 8 else devices
        sizes.append(size)
        devices //= size
    return sizes


def digit_shift(array, stride, size, by, devices):
    pairs = []
    for i in range(devices):
        digit = i // stride % size
        pairs.append((i, i + ((digit ^ by) - digit) * stride))
    return lax.ppermute(array, "dp", pairs)


def reduce_over_replicas(scal, arrays, devices):
    sizes = stage_sizes(devices)
    stride = 1
    for place, size in enumerate(sizes):
        blocks = scatter_sums(scal, arrays, place + 1, size)
        arrays = [blocks[0]]
        for j in range(1, size):
            arrays.append(digit_shift(blocks[j], stride, size, j, devices))
        stride *= size
    chunk = scatter_sums(scal, arrays, 0, 1)[0]
    for place in reversed(range(len(sizes))):
        size = sizes[place]
        stride //= size
        pieces = [chunk] + [digit_shift(chunk, stride, size, j, devices) for j in range(1, size)]
        if place:
            shape = (chunk.shape[0] * size, BLOCK)
            chunk = single_step(
                functools.partial(gather_kernel, place + 1), scal, pieces, [(shape, low)]
            )[0]
    return pieces


def per_device(
    activations,
    cotangent,
    segment_ids,
    pad_mask,
    norm1_gain,
    norm1_bias,
    qkv_weight,
    qv_bias,
    out_weight,
    out_bias,
    norm2_gain,
    norm2_bias,
    up_weight,
    up_bias,
    down_weight,
    down_bias,
):
    devices = lax.axis_size("dp")
    replica = lax.axis_index("dp")
    digits, stride = [], 1
    for size in stage_sizes(devices):
        digits.append(replica // stride % size)
        stride *= size
    scal = jnp.stack([lax.axis_index("section")] + digits).astype(jnp.int32)
    local_rows, slots, width = activations.shape
    hidden_width = up_weight.shape[-1]
    tokens = local_rows // 2 * slots

    vec_rows = 8 + hidden_width // width
    vec = pl.pallas_call(
        pack_kernel, out_shape=jax.ShapeDtypeStruct((vec_rows, width), full)
    )(norm1_gain, norm1_bias, qv_bias, out_bias, norm2_gain, norm2_bias, up_bias, down_bias)
    own = (qkv_weight[0], out_weight[0], up_weight[0], down_weight[0], vec)
    other = tuple(lax.ppermute(w, "section", SWAP) for w in own)
    attn_own, attn_other = (own[0], own[1], own[4]), (other[0], other[1], other[4])
    ffn_own, ffn_other = own[2:], other[2:]

    x = activations.reshape(-1, width)
    seed = cotangent.reshape(-1, width)

    first, *kept1 = run_forward(
        0, scal, x, True, segment_ids, pad_mask, own, other, tokens, slots
    )
    outs_send, outs_mine, *kept2 = run_forward(
        1, scal, first, False, segment_ids, pad_mask, own, other, tokens, slots
    )
    outs_got = lax.ppermute(outs_send, "section", SWAP)

    dres2, ffn2_keep, ffn2_send = run_ffn_backward(
        1, scal, seed, True, pad_mask, kept2[4:], ffn_own, ffn_other, tokens, slots, devices
    )
    ffn2_got = lax.ppermute(ffn2_send, "section", SWAP)
    dx2, attn2_keep, attn2_send = run_attention_backward(
        1, scal, first, False, [dres2] + kept2[:4], None, attn_own, attn_other, tokens, slots, devices
    )
    attn2_got = lax.ppermute(attn2_send, "section", SWAP)
    ffn2 = lax.psum(ffn2_keep + ffn2_got, "dp")
    dres1, ffn1_keep, ffn1_send = run_ffn_backward(
        0, scal, dx2, False, pad_mask, kept1[4:], ffn_own, ffn_other, tokens, slots, devices
    )
    ffn1_got = lax.ppermute(ffn1_send, "section", SWAP)
    attn2_sum, ffn2 = lax.optimization_barrier((attn2_keep + attn2_got, ffn2))
    attn2 = lax.psum(attn2_sum, "dp")
    grads_send, grads_mine, attn1_keep, attn1_send = run_attention_backward(
        0, scal, x, True, [dres1] + kept1[:4], dx2, attn_own, attn_other, tokens, slots, devices
    )
    attn1_got = lax.ppermute(attn1_send, "section", SWAP)
    grads_got = lax.ppermute(grads_send, "section", SWAP)

    ffn1 = reduce_over_replicas(scal, [ffn1_keep, ffn1_got], devices)
    attn1 = reduce_over_replicas(scal, [attn1_keep, attn1_got], devices)

    def finish(pieces, second, shapes, smalls):
        lacking = single_step(
            functools.partial(choose_kernel, 1), scal, pieces + [second], [(second.shape, low)]
        )[0]
        got = lax.ppermute(lacking, "section", SWAP)
        results = [((1,) + shape, full) for shape in shapes] + [((1, n), full) for n in smalls]
        return single_step(
            functools.partial(unpack_kernel, 1, len(pieces), shapes, smalls),
            scal,
            pieces + [second, got],
            results,
            [pltpu.VMEM(second.shape, low)],
        )

    down_grad, up_grad, up_b, down_b, gain2, shift2 = finish(
        ffn1,
        ffn2,
        [(hidden_width, width), (width, hidden_width)],
        [hidden_width, width, width, width],
    )
    qkv_grad, out_grad, qv_b, out_b, gain1, shift1 = finish(
        attn1, attn2, [(width, 3 * width), (width, width)], [2 * width, width, width, width]
    )
    layer_outs = fill_other_half(scal, outs_mine, outs_got, 4)
    layer_in_grads = fill_other_half(scal, grads_mine, grads_got, 4)
    shape = (1, local_rows, slots, width)
    return (
        layer_outs.reshape(shape),
        layer_in_grads.reshape(shape),
        gain1,
        shift1,
        qkv_grad,
        qv_b,
        out_grad,
        out_b,
        gain2,
        shift2,
        up_grad,
        up_b,
        down_grad,
        down_b,
    )


def solution(mesh):
    in_specs = (
        P("dp", None, None),
        P("dp", None, None),
        P("dp", None),
        P("dp", None),
        P("section", None),
        P("section", None),
        P("section", None, None),
        P("section", None),
        P("section", None, None),
        P("section", None),
        P("section", None),
        P("section", None),
        P("section", None, None),
        P("section", None),
        P("section", None, None),
        P("section", None),
    )
    out_specs = (
        P("section", "dp", None, None),
        P("section", "dp", None, None),
        P("section", None),
        P("section", None),
        P("section", None, None),
        P("section", None),
        P("section", None, None),
        P("section", None),
        P("section", None),
        P("section", None),
        P("section", None, None),
        P("section", None),
        P("section", None, None),
        P("section", None),
    )
    return jax.shard_map(
        per_device, mesh=mesh, in_specs=in_specs, out_specs=out_specs, check_vma=False
    )
```

```python
import functools

import jax
import jax.numpy as jnp
from jax import lax
from jax.experimental import pallas as pl
from jax.experimental.pallas import tpu as pltpu
from jax.sharding import PartitionSpec as P

H = 6
R_F, R_FB, R_AB = 2, 4, 4
BLOCK = 128
norm_eps = 1e-06
forbidden = -1e30
sqrt_half = 0.7071067811865476
inverse_root_two_pi = 0.3989422804014327
VMEM_LIMIT = 60 * 1024 * 1024
low = jnp.bfloat16
full = jnp.float32


def nn(a, b):
    return lax.dot_general(a, b, (((1,), (0,)), ((), ())), preferred_element_type=full)


def nt(a, b):
    return lax.dot_general(a, b, (((1,), (1,)), ((), ())), preferred_element_type=full)


def tn(a, b):
    return lax.dot_general(a, b, (((0,), (0,)), ((), ())), preferred_element_type=full)


def column_blocks(width, step):
    return [(start, min(start + step, width)) for start in range(0, width, step)]


def fold_rows(values):
    return jnp.sum(values.reshape(values.shape[0] // 8, 8, values.shape[1]), axis=0)


def gelu_parts(hidden):
    size = jnp.abs(hidden)
    t = pl.reciprocal(1.0 + (0.3275911 * sqrt_half) * size, approx=True)
    bell = jnp.exp(-0.5 * (hidden * hidden))
    series = t * (
        0.127414796
        + t * (-0.142248368 + t * (0.7107068705 + t * (-0.7265760135 + t * 0.5307027145)))
    )
    tail = series * bell
    cdf = jnp.where(hidden >= 0.0, 1.0 - tail, tail)
    return (hidden * cdf, cdf + (hidden * inverse_root_two_pi) * bell)


def norm_parts(values):
    average = jnp.mean(values, axis=-1, keepdims=True)
    centred = values - average
    inverse = lax.rsqrt(jnp.mean(centred * centred, axis=-1, keepdims=True) + norm_eps)
    return (centred * inverse, inverse)


def head_lanes():
    lane = lax.broadcasted_iota(jnp.int32, (1, BLOCK), 1)
    first = jnp.where(lane < BLOCK // 2, 1.0, 0.0)
    return (first.astype(low), (1.0 - first).astype(low))


def fetch_weights(scal_ref, layer, own, other, held, sems):
    @pl.when(pl.program_id(0) == 0)
    def _():
        @pl.when(scal_ref[0] == layer)
        def _():
            for i in range(len(own)):
                pltpu.make_async_copy(own[i], held[i], sems.at[i]).start()

        @pl.when(scal_ref[0] != layer)
        def _():
            for i in range(len(own)):
                pltpu.make_async_copy(other[i], held[i], sems.at[i]).start()

        for i in range(len(own)):
            pltpu.make_async_copy(own[i], held[i], sems.at[i]).wait()


def row_index(scal_ref, steps_rows, r):
    return (scal_ref[0] * pl.num_programs(0) + pl.program_id(0)) * steps_rows + r


def pack_kernel(g1, b1, qv, ob, g2, b2, ub, db, out_ref):
    width = g1.shape[1]
    rows = [g1[...], b1[...], qv[:, :width], qv[:, width:], ob[...], g2[...], b2[...], db[...]]
    rows += [ub[:, c : c + width] for c in range(0, ub.shape[1], width)]
    out_ref[...] = jnp.concatenate(rows, axis=0)


def forward_kernel(layer, slots, scal_ref, x_ref, seg_ref, pad_ref, *rest):
    own, other = rest[0:5], rest[5:10]
    rest = rest[10:]
    if layer == 0:
        out_ref, rest = rest[0], rest[1:]
    else:
        send_ref, mine_ref, rest = rest[0], rest[1], rest[2:]
    qkv_ref, e_ref, rinv_ref, mixed_ref, xhat_ref, inv_ref, act_ref, slope_ref = rest[:8]
    wqkv, wout, wup, wdown, vec, na_s, res_s, nb_s, sg_s, bk_s, va_s, sems = rest[8:]
    fetch_weights(scal_ref, layer, own, other, (wqkv, wout, wup, wdown, vec), sems)
    tokens, width = x_ref.shape
    hidden_width = wup.shape[1]
    step = 64
    gain_a, shift_a = vec[0:1, :], vec[1:2, :]
    q_off, v_off = vec[2:3, :], vec[3:4, :]
    out_off, gain_b, shift_b, down_off = (vec[i : i + 1, :] for i in range(4, 8))
    for t in range(0, tokens, step):
        scaled, _ = norm_parts(x_ref[t : t + step, :].astype(full))
        na_s[t : t + step, :] = (scaled * gain_a + shift_a).astype(low)
    code = lax.broadcasted_iota(jnp.int32, (BLOCK, slots), 0)
    for r in range(tokens // slots):
        rows = slice(r * slots, (r + 1) * slots)
        row = row_index(scal_ref, tokens // slots, r)
        same = seg_ref[pl.ds(row, 1), :] == code
        pad = pad_ref[pl.ds(row, 1), :]
        sg_s[rows, :] = jnp.where(same, 1.0, 0.0).T.astype(low)
        bk_s[rows, :] = jnp.where(same & (pad > 0), 0.0, forbidden).T.astype(low)
        va_s[rows, :] = jnp.broadcast_to(pad.astype(full), (BLOCK, slots)).T
    for n0, n1 in column_blocks(3 * width, 512):
        part = nn(na_s[...], wqkv[:, n0:n1])
        for c in range(n0, n1, BLOCK):
            piece = part[:, c - n0 : c - n0 + BLOCK]
            if c < width:
                piece = (piece + q_off[:, c : c + BLOCK]) * 0.125
            elif c >= 2 * width:
                piece = piece + v_off[:, c - 2 * width : c - 2 * width + BLOCK]
            qkv_ref[:, c : c + BLOCK] = piece.astype(low)
    lanes = head_lanes()
    ones = jnp.ones((slots, BLOCK), low)
    for r in range(tokens // slots):
        rows = slice(r * slots, (r + 1) * slots)
        for p in range(H // 2):
            q2 = qkv_ref[rows, p * BLOCK : (p + 1) * BLOCK]
            k2 = qkv_ref[rows, width + p * BLOCK : width + (p + 1) * BLOCK]
            v2 = qkv_ref[rows, 2 * width + p * BLOCK : 2 * width + (p + 1) * BLOCK]
            keys = jnp.concatenate([k2, bk_s[rows, :]], axis=1)
            weights = []
            for i in range(2):
                queries = jnp.concatenate([q2 * lanes[i], sg_s[rows, :]], axis=1)
                scores = nt(queries, keys)
                e = jnp.exp(scores - jnp.max(scores, axis=1, keepdims=True)).astype(low)
                e_ref[rows, (2 * p + i) * slots : (2 * p + i + 1) * slots] = e
                weights.append(e)
            values = jnp.concatenate(
                [
                    jnp.concatenate([v2 * lanes[0], ones * lanes[0]], axis=1),
                    jnp.concatenate([v2 * lanes[1], ones * lanes[1]], axis=1),
                ],
                axis=0,
            )
            both = nn(jnp.concatenate(weights, axis=1), values)
            rinv = 1.0 / both[:, BLOCK:]
            rinv_ref[rows, p * BLOCK : (p + 1) * BLOCK] = rinv
            mixed_ref[rows, p * BLOCK : (p + 1) * BLOCK] = (both[:, :BLOCK] * rinv).astype(low)
    res_s[...] = x_ref[...].astype(full) + (nn(mixed_ref[...], wout[...]) + out_off)
    for t in range(0, tokens, step):
        scaled, inverse = norm_parts(res_s[t : t + step, :])
        xhat_ref[t : t + step, :] = scaled.astype(low)
        inv_ref[t : t + step, :] = jnp.broadcast_to(inverse, (step, BLOCK))
        nb_s[t : t + step, :] = (scaled * gain_b + shift_b).astype(low)
    for n0, n1 in column_blocks(hidden_width, 256):
        offset = jnp.concatenate(
            [
                vec[8 + c // width : 9 + c // width, c % width : c % width + BLOCK]
                for c in range(n0, n1, BLOCK)
            ],
            axis=1,
        )
        act, slope = gelu_parts(nn(nb_s[...], wup[:, n0:n1]) + offset)
        act_ref[:, n0:n1] = act.astype(low)
        slope_ref[:, n0:n1] = slope.astype(low)
    outcome = res_s[...] + (nn(act_ref[...], wdown[...]) + down_off)
    for c in range(0, width, BLOCK):
        piece = (va_s[...] * outcome[:, c : c + BLOCK]).astype(low)
        if layer == 0:
            out_ref[:, c : c + BLOCK] = piece
        else:
            before = x_ref[:, c : c + BLOCK]

            @pl.when(scal_ref[0] == 0)
            def _():
                send_ref[:, c : c + BLOCK] = piece
                mine_ref[:, c : c + BLOCK] = before

            @pl.when(scal_ref[0] != 0)
            def _():
                send_ref[:, c : c + BLOCK] = before
                mine_ref[:, c : c + BLOCK] = piece


def small_block(vectors):
    row = jnp.concatenate([jnp.sum(v, axis=0, keepdims=True) for v in vectors], axis=1)
    count = row.shape[1] // BLOCK
    pieces = [row[:, j * BLOCK : (j + 1) * BLOCK] for j in range(count)]
    padded = -(-count // 16) * 16
    if padded > count:
        pieces.append(jnp.zeros((padded - count, BLOCK), full))
    return jnp.concatenate(pieces, axis=0).astype(low)


def store_payload(scal_ref, keep_ref, send_ref, write):
    for h in range(2):

        @pl.when(scal_ref[0] == h)
        def _():
            write(keep_ref, h)

        @pl.when(scal_ref[0] != h)
        def _():
            write(send_ref, h)


def store_columns(ref, base, matrix, row0, rows):
    for b in range(matrix.shape[1] // BLOCK):
        ref[base + b * rows : base + (b + 1) * rows, :] = matrix[
            row0 : row0 + rows, b * BLOCK : (b + 1) * BLOCK
        ].astype(low)
    return base + rows * (matrix.shape[1] // BLOCK)


def store_rest(ref, base, block):
    ref[base : base + block.shape[0], :] = block
    base += block.shape[0]
    if base < ref.shape[0]:
        ref[base:, :] = jnp.zeros((ref.shape[0] - base, BLOCK), low)


def ffn_backward_kernel(
    layer, slots, scal_ref, dy_ref, xhat_ref, inv_ref, act_ref, slope_ref, pad_ref, *rest
):
    own, other = rest[0:3], rest[3:6]
    dres_ref, keep_ref, send_ref = rest[6:9]
    wup, wdown, vec, dd_s, ddt_s, nbt_s, dh_s, dnb_s, accd, accu, su, sd, sg, sb, sems = rest[9:]
    fetch_weights(scal_ref, layer, own, other, (wup, wdown, vec), sems)
    tokens, width = dy_ref.shape
    hidden_width = wup.shape[1]
    step = 64

    @pl.when(pl.program_id(0) == 0)
    def _():
        for ref in (accd, accu, su, sd, sg, sb):
            ref[...] = jnp.zeros_like(ref)

    gain_b, shift_b = vec[5:6, :], vec[6:7, :]
    for r in range(tokens // slots):
        rows = slice(r * slots, (r + 1) * slots)
        row = row_index(scal_ref, tokens // slots, r)
        pad = pad_ref[pl.ds(row, 1), :].astype(full)
        valid = jnp.broadcast_to(pad, (BLOCK, slots)).T.astype(low)
        for c in range(0, width, BLOCK):
            dd_s[rows, c : c + BLOCK] = dy_ref[rows, c : c + BLOCK] * valid
    ddt_s[...] = dd_s[...].T
    sd[...] += fold_rows(dd_s[...].astype(full))
    nbt_s[...] = (xhat_ref[...].astype(full) * gain_b + shift_b).astype(low).T
    for n0, n1 in column_blocks(hidden_width, 256):
        back = nt(dd_s[...], wdown[n0:n1, :])
        dh = (back * slope_ref[:, n0:n1].astype(full)).astype(low)
        dh_s[:, n0:n1] = dh
        su[:, n0:n1] += fold_rows(dh.astype(full))
        accd[:, n0:n1] += nn(ddt_s[...], act_ref[:, n0:n1])
        accu[:, n0:n1] += nn(nbt_s[...], dh)
    dnb_s[...] = nt(dh_s[...], wup[...])
    for t in range(0, tokens, step):
        scaled = xhat_ref[t : t + step, :].astype(full)
        inverse = inv_ref[t : t + step, :]
        inverse = jnp.concatenate([inverse] * (width // BLOCK), axis=1)
        dn = dnb_s[t : t + step, :]
        sg[...] += fold_rows(dn * scaled)
        sb[...] += fold_rows(dn)
        e = dn * gain_b
        inner = (e - jnp.mean(e, axis=-1, keepdims=True)) - scaled * jnp.mean(
            e * scaled, axis=-1, keepdims=True
        )
        dres_ref[t : t + step, :] = dd_s[t : t + step, :].astype(full) + inverse * inner

    @pl.when(pl.program_id(0) == pl.num_programs(0) - 1)
    def _():
        small = small_block([su[...], sd[...], sg[...], sb[...]])

        def write(ref, h):
            half = hidden_width // 2
            for b in range(width // BLOCK):
                turned = accd[b * BLOCK : (b + 1) * BLOCK, h * half : (h + 1) * half].T
                ref[b * half : (b + 1) * half, :] = turned.astype(low)
            base = store_columns(ref, half * (width // BLOCK), accu, h * width // 2, width // 2)
            store_rest(ref, base, small)

        store_payload(scal_ref, keep_ref, send_ref, write)


def attention_backward_kernel(
    layer, slots, scal_ref, x_ref, dres_ref, qkv_ref, e_ref, rinv_ref, mixed_ref, *rest
):
    if layer == 0:
        later_ref, rest = rest[0], rest[1:]
    own, other, rest = rest[0:3], rest[3:6], rest[6:]
    if layer == 0:
        dsend_ref, dmine_ref, rest = rest[0], rest[1], rest[2:]
    else:
        dx_ref, rest = rest[0], rest[1:]
    keep_ref, send_ref = rest[0:2]
    wqkv, wout, vec, db_s, mixt_s, do_s, pr_s, dp_s, xh_s, iv_s, nat_s, dna_s = rest[2:14]
    accq, acco, sq, so, sg, sb, sems = rest[14:]
    fetch_weights(scal_ref, layer, own, other, (wqkv, wout, vec), sems)
    tokens, width = x_ref.shape
    step = 64

    @pl.when(pl.program_id(0) == 0)
    def _():
        for ref in (accq, acco, sq, so, sg, sb):
            ref[...] = jnp.zeros_like(ref)

    gain_a, shift_a = vec[0:1, :], vec[1:2, :]
    db_s[...] = dres_ref[...].astype(low)
    so[...] += fold_rows(db_s[...].astype(full))
    mixt_s[...] = mixed_ref[...].T
    acco[...] += nn(mixt_s[...], db_s[...])
    scaled_do = nt(db_s[...], wout[...]) * rinv_ref[...]
    do_s[...] = scaled_do.astype(low)
    pr_s[...] = (scaled_do * (-mixed_ref[...].astype(full))).astype(low)
    for t in range(0, tokens, step):
        scaled, inverse = norm_parts(x_ref[t : t + step, :].astype(full))
        xh_s[t : t + step, :] = scaled
        iv_s[t : t + step, :] = jnp.broadcast_to(inverse, (step, BLOCK))
        dna_s[t : t + step, :] = scaled * gain_a + shift_a
    nat_s[...] = dna_s[...].astype(low).T
    lanes = head_lanes()
    ones = jnp.ones((slots, BLOCK), low)
    for r in range(tokens // slots):
        rows = slice(r * slots, (r + 1) * slots)
        for p in range(H // 2):
            cols = slice(p * BLOCK, (p + 1) * BLOCK)
            q2 = qkv_ref[rows, p * BLOCK : (p + 1) * BLOCK]
            k2 = qkv_ref[rows, width + p * BLOCK : width + (p + 1) * BLOCK]
            v2 = qkv_ref[rows, 2 * width + p * BLOCK : 2 * width + (p + 1) * BLOCK]
            do2, pr2 = do_s[rows, cols], pr_s[rows, cols]
            values = jnp.concatenate([v2, ones], axis=1)
            weights, slopes, dos, qs, ks = [], [], [], [], []
            for i in range(2):
                e = e_ref[rows, (2 * p + i) * slots : (2 * p + i + 1) * slots]
                do = do2 * lanes[i]
                inner = nt(jnp.concatenate([do, pr2 * lanes[i]], axis=1), values)
                slopes.append((e.astype(full) * inner).astype(low))
                weights.append(e)
                dos.append(do)
                qs.append(q2 * lanes[i])
                ks.append(k2 * lanes[i])
            dv = tn(jnp.concatenate(weights, axis=0), jnp.concatenate(dos, axis=0))
            dk = tn(jnp.concatenate(slopes, axis=0), jnp.concatenate(qs, axis=0))
            dq = nn(jnp.concatenate(slopes, axis=1), jnp.concatenate(ks, axis=0)) * 0.125
            dp_s[rows, p * BLOCK : (p + 1) * BLOCK] = dq.astype(low)
            dp_s[rows, width + p * BLOCK : width + (p + 1) * BLOCK] = dk.astype(low)
            dp_s[rows, 2 * width + p * BLOCK : 2 * width + (p + 1) * BLOCK] = dv.astype(low)
    sq[:, :width] += fold_rows(dp_s[:, :width].astype(full))
    sq[:, width:] += fold_rows(dp_s[:, 2 * width :].astype(full))
    for n0, n1 in column_blocks(3 * width, 512):
        accq[:, n0:n1] += nn(nat_s[...], dp_s[:, n0:n1])
    dna_s[...] = nt(dp_s[...], wqkv[...])
    for t in range(0, tokens, step):
        part = slice(t, t + step)
        scaled = xh_s[part, :]
        inverse = iv_s[part, :]
        inverse = jnp.concatenate([inverse] * (width // BLOCK), axis=1)
        dn = dna_s[part, :]
        sg[...] += fold_rows(dn * scaled)
        sb[...] += fold_rows(dn)
        e = dn * gain_a
        inner = (e - jnp.mean(e, axis=-1, keepdims=True)) - scaled * jnp.mean(
            e * scaled, axis=-1, keepdims=True
        )
        dna_s[part, :] = dres_ref[part, :] + inverse * inner
    if layer == 0:

        @pl.when(scal_ref[0] == 0)
        def _():
            dmine_ref[...] = dna_s[...]
            dsend_ref[...] = later_ref[...]

        @pl.when(scal_ref[0] != 0)
        def _():
            dmine_ref[...] = later_ref[...].astype(full)
            dsend_ref[...] = dna_s[...].astype(low)

    else:
        dx_ref[...] = dna_s[...].astype(low)

    @pl.when(pl.program_id(0) == pl.num_programs(0) - 1)
    def _():
        small = small_block([sq[...], so[...], sg[...], sb[...]])

        def write(ref, h):
            base = store_columns(ref, 0, accq, h * width // 2, width // 2)
            base = store_columns(ref, base, acco, h * width // 2, width // 2)
            store_rest(ref, base, small)

        store_payload(scal_ref, keep_ref, send_ref, write)


def call_kernel(kernel, scal, steps, blocked, fixed, hbm, outs, fixed_outs, scratch, flops, moved):
    own_index = lambda i, s: (i, 0)
    shared_index = lambda i, s: (s[0] * steps + i, 0)

    def spec(shape, shared):
        rows = shape[0] // (2 * steps if shared else steps)
        return pl.BlockSpec((rows, shape[1]), shared_index if shared else own_index)

    in_specs, args = [], []
    for array, shared in blocked:
        in_specs.append(spec(array.shape, shared))
        args.append(array)
    for array in fixed:
        in_specs.append(pl.BlockSpec(array.shape, lambda i, s, n=array.ndim: (0,) * n))
        args.append(array)
    for array in hbm:
        in_specs.append(pl.BlockSpec(memory_space=pl.ANY))
        args.append(array)
    out_specs, out_shapes = [], []
    for shape, dtype, shared in outs:
        out_specs.append(spec(shape, shared))
        out_shapes.append(jax.ShapeDtypeStruct(shape, dtype))
    for shape, dtype in fixed_outs:
        out_specs.append(pl.BlockSpec(shape, lambda i, s, n=len(shape): (0,) * n))
        out_shapes.append(jax.ShapeDtypeStruct(shape, dtype))
    return pl.pallas_call(
        kernel,
        grid_spec=pltpu.PrefetchScalarGridSpec(
            num_scalar_prefetch=1,
            grid=(steps,),
            in_specs=in_specs,
            out_specs=out_specs,
            scratch_shapes=scratch,
        ),
        out_shape=out_shapes,
        compiler_params=pltpu.CompilerParams(vmem_limit_bytes=VMEM_LIMIT),
        cost_estimate=pl.CostEstimate(flops=flops, bytes_accessed=moved, transcendentals=0),
    )(scal, *args)


def run_forward(layer, scal, x, shared, segments, pad, own, other, tokens, slots):
    width = x.shape[1]
    hidden_width = own[2].shape[1]
    steps = tokens // (R_F * slots)
    per_step = R_F * slots
    if layer == 0:
        outs = [((tokens, width), low, False)]
    else:
        outs = [((tokens, width), low, False), ((2 * tokens, width), low, True)]
    outs += [
        ((tokens, 3 * width), low, False),
        ((tokens, H * slots), low, False),
        ((tokens, width), full, False),
        ((tokens, width), low, False),
        ((tokens, width), low, False),
        ((tokens, BLOCK), full, False),
        ((tokens, hidden_width), low, False),
        ((tokens, hidden_width), low, False),
    ]
    scratch = [pltpu.VMEM(w.shape, w.dtype) for w in own] + [
        pltpu.VMEM((per_step, width), low),
        pltpu.VMEM((per_step, width), full),
        pltpu.VMEM((per_step, width), low),
        pltpu.VMEM((per_step, BLOCK), low),
        pltpu.VMEM((per_step, BLOCK), low),
        pltpu.VMEM((per_step, BLOCK), full),
        pltpu.SemaphoreType.DMA((5,)),
    ]
    return call_kernel(
        functools.partial(forward_kernel, layer, slots),
        scal,
        steps,
        [(x, shared)],
        [segments, pad],
        list(own) + list(other),
        outs,
        [],
        scratch,
        2 * tokens * (4 * width * width + 2 * width * hidden_width + 2 * slots * width),
        tokens * 14000,
    )


def payload_rows(used, devices):
    unit = devices * 16
    return -(-used // unit) * unit


def run_ffn_backward(layer, scal, dy, shared, pad, saved, own, other, tokens, slots, devices):
    width, hidden_width = own[0].shape
    steps = tokens // (R_FB * slots)
    per_step = R_FB * slots
    rows = payload_rows(hidden_width * width // BLOCK + 32, devices)
    scratch = [pltpu.VMEM(w.shape, w.dtype) for w in own] + [
        pltpu.VMEM((per_step, width), low),
        pltpu.VMEM((width, per_step), low),
        pltpu.VMEM((width, per_step), low),
        pltpu.VMEM((per_step, hidden_width), low),
        pltpu.VMEM((per_step, width), full),
        pltpu.VMEM((width, hidden_width), full),
        pltpu.VMEM((width, hidden_width), full),
        pltpu.VMEM((8, hidden_width), full),
        pltpu.VMEM((8, width), full),
        pltpu.VMEM((8, width), full),
        pltpu.VMEM((8, width), full),
        pltpu.SemaphoreType.DMA((3,)),
    ]
    return call_kernel(
        functools.partial(ffn_backward_kernel, layer, slots),
        scal,
        steps,
        [(dy, shared)] + [(array, False) for array in saved],
        [pad],
        list(own) + list(other),
        [((tokens, width), full, False)],
        [((rows, BLOCK), low), ((rows, BLOCK), low)],
        scratch,
        8 * tokens * width * hidden_width,
        tokens * 10000,
    )


def run_attention_backward(layer, scal, x, shared, saved, later, own, other, tokens, slots, devices):
    width = x.shape[1]
    steps = tokens // (R_AB * slots)
    per_step = R_AB * slots
    rows = payload_rows(2 * width * width // BLOCK + 16, devices)
    blocked = [(x, shared)] + [(array, False) for array in saved]
    if layer == 0:
        blocked.append((later, False))
        outs = [((tokens, width), low, False), ((2 * tokens, width), full, True)]
    else:
        outs = [((tokens, width), low, False)]
    scratch = [pltpu.VMEM(w.shape, w.dtype) for w in own] + [
        pltpu.VMEM((per_step, width), low),
        pltpu.VMEM((width, per_step), low),
        pltpu.VMEM((per_step, width), low),
        pltpu.VMEM((per_step, width), low),
        pltpu.VMEM((per_step, 3 * width), low),
        pltpu.VMEM((per_step, width), full),
        pltpu.VMEM((per_step, BLOCK), full),
        pltpu.VMEM((width, per_step), low),
        pltpu.VMEM((per_step, width), full),
        pltpu.VMEM((width, 3 * width), full),
        pltpu.VMEM((width, width), full),
        pltpu.VMEM((8, 2 * width), full),
        pltpu.VMEM((8, width), full),
        pltpu.VMEM((8, width), full),
        pltpu.VMEM((8, width), full),
        pltpu.SemaphoreType.DMA((3,)),
    ]
    return call_kernel(
        functools.partial(attention_backward_kernel, layer, slots),
        scal,
        steps,
        blocked,
        [],
        list(own) + list(other),
        outs,
        [((rows, BLOCK), low), ((rows, BLOCK), low)],
        scratch,
        2 * tokens * (8 * width * width + 5 * slots * width),
        tokens * 11000,
    )


def fill_kernel(scal_ref, got_ref, held_ref, out_ref):
    del scal_ref, held_ref
    out_ref[...] = got_ref[...].astype(out_ref.dtype)


def fill_other_half(scal, held, got, steps):
    rows = got.shape[0] // steps
    return pl.pallas_call(
        fill_kernel,
        grid_spec=pltpu.PrefetchScalarGridSpec(
            num_scalar_prefetch=1,
            grid=(steps,),
            in_specs=[
                pl.BlockSpec((rows, got.shape[1]), lambda i, s: (i, 0)),
                pl.BlockSpec(memory_space=pl.ANY),
            ],
            out_specs=pl.BlockSpec(
                (rows, got.shape[1]), lambda i, s: ((1 - s[0]) * steps + i, 0)
            ),
        ),
        out_shape=jax.ShapeDtypeStruct(held.shape, held.dtype),
        input_output_aliases={2: 0},
        cost_estimate=pl.CostEstimate(
            flops=0, bytes_accessed=8 * got.size, transcendentals=0
        ),
    )(scal, got, held)


def single_step(kernel, scal, arrays, shapes, scratch=()):
    whole = lambda shape: pl.BlockSpec(shape, lambda i, s, n=len(shape): (0,) * n)
    moved = sum(a.size * a.dtype.itemsize for a in arrays)
    return pl.pallas_call(
        kernel,
        grid_spec=pltpu.PrefetchScalarGridSpec(
            num_scalar_prefetch=1,
            grid=(1,),
            in_specs=[whole(a.shape) for a in arrays],
            out_specs=[whole(shape) for shape, _ in shapes],
            scratch_shapes=list(scratch),
        ),
        out_shape=[jax.ShapeDtypeStruct(shape, dtype) for shape, dtype in shapes],
        compiler_params=pltpu.CompilerParams(vmem_limit_bytes=VMEM_LIMIT),
        cost_estimate=pl.CostEstimate(flops=0, bytes_accessed=3 * moved, transcendentals=0),
    )(scal, *arrays)


def unpack_kernel(shapes, smalls, scal_ref, first, second, got, *refs):
    matrices, vectors = refs[: len(shapes)], refs[len(shapes) :]

    def write(source, h):
        base = 0
        for (rows, columns), out_ref in zip(shapes, matrices):
            half = rows // 2
            for b in range(columns // BLOCK):
                out_ref[0, h * half : (h + 1) * half, b * BLOCK : (b + 1) * BLOCK] = source[
                    base : base + half, :
                ].astype(full)
                base += half

    @pl.when(scal_ref[0] == 0)
    def _():
        write(first, 0)
        write(got, 1)

    @pl.when(scal_ref[0] != 0)
    def _():
        write(got, 0)
        write(second, 1)

    base = sum(rows // 2 * columns // BLOCK for rows, columns in shapes)
    padded = -(-sum(smalls) // BLOCK // 16) * 16
    block = got[base : base + padded, :].astype(full)
    row = 0
    for size, out_ref in zip(smalls, vectors):
        for c in range(0, size, BLOCK):
            out_ref[0:1, c : c + BLOCK] = block[row : row + 1, :]
            row += 1


SWAP = [(0, 1), (1, 0)]


def stage_sizes(devices):
    sizes = []
    while devices > 1:
        size = 4 if devices % 4 == 0 and devices != 8 else devices
        sizes.append(size)
        devices //= size
    return sizes


def exchange(blocks, place, devices):
    sizes = stage_sizes(devices)
    stride = 1
    for size in sizes[:place]:
        stride *= size
    size = sizes[place]
    groups = []
    for start in range(devices):
        if start // stride % size == 0:
            groups.append([start + k * stride for k in range(size)])
    return lax.all_to_all(blocks, "dp", 0, 0, axis_index_groups=groups)


def scatter_stage(array, place, devices):
    size = stage_sizes(devices)[place]
    return exchange(array.reshape(size, -1, BLOCK), place, devices)


def gather_stage(array, place, devices):
    size = stage_sizes(devices)[place]
    copies = jnp.broadcast_to(array[None], (size,) + array.shape)
    return exchange(copies, place, devices).reshape(-1, BLOCK)


def add_up(blocks):
    return jnp.sum(blocks.astype(full), axis=0).astype(low)


def pair_sum(keep, send):
    got = lax.ppermute(send, "section", SWAP)
    return (keep.astype(full) + got.astype(full)).astype(low)


together = lax.optimization_barrier


def per_device(
    activations,
    cotangent,
    segment_ids,
    pad_mask,
    norm1_gain,
    norm1_bias,
    qkv_weight,
    qv_bias,
    out_weight,
    out_bias,
    norm2_gain,
    norm2_bias,
    up_weight,
    up_bias,
    down_weight,
    down_bias,
):
    devices = lax.axis_size("dp")
    scal = lax.axis_index("section").astype(jnp.int32).reshape(1)
    local_rows, slots, width = activations.shape
    hidden_width = up_weight.shape[-1]
    tokens = local_rows // 2 * slots

    vec_rows = 8 + hidden_width // width
    vec = pl.pallas_call(
        pack_kernel, out_shape=jax.ShapeDtypeStruct((vec_rows, width), full)
    )(norm1_gain, norm1_bias, qv_bias, out_bias, norm2_gain, norm2_bias, up_bias, down_bias)
    own = (qkv_weight[0], out_weight[0], up_weight[0], down_weight[0], vec)
    other = tuple(lax.ppermute(w, "section", SWAP) for w in own)
    attn_own, attn_other = (own[0], own[1], own[4]), (other[0], other[1], other[4])
    ffn_own, ffn_other = own[2:], other[2:]

    x = activations.reshape(-1, width)
    seed = cotangent.reshape(-1, width)

    first, *kept1 = run_forward(
        0, scal, x, True, segment_ids, pad_mask, own, other, tokens, slots
    )
    outs_send, outs_mine, *kept2 = run_forward(
        1, scal, first, False, segment_ids, pad_mask, own, other, tokens, slots
    )
    outs_got = lax.ppermute(outs_send, "section", SWAP)

    dres2, ffn2_keep, ffn2_send = run_ffn_backward(
        1, scal, seed, True, pad_mask, kept2[4:], ffn_own, ffn_other, tokens, slots, devices
    )
    stages = list(range(len(stage_sizes(devices))))
    last = stages[-1]
    ffn2 = pair_sum(ffn2_keep, ffn2_send)
    dres2, ffn2 = together((dres2, ffn2))
    ffn2 = scatter_stage(ffn2, 0, devices)
    dx2, attn2_keep, attn2_send = run_attention_backward(
        1, scal, first, False, [dres2] + kept2[:4], None, attn_own, attn_other, tokens, slots, devices
    )
    attn2 = pair_sum(attn2_keep, attn2_send)
    dx2, attn2, ffn2 = together((dx2, attn2, add_up(ffn2)))
    attn2 = scatter_stage(attn2, 0, devices)
    for place in stages[1:-1]:
        ffn2 = add_up(scatter_stage(ffn2, place, devices))
    ffn2 = scatter_stage(ffn2, last, devices)
    dres1, ffn1_keep, ffn1_send = run_ffn_backward(
        0, scal, dx2, False, pad_mask, kept1[4:], ffn_own, ffn_other, tokens, slots, devices
    )
    ffn1 = pair_sum(ffn1_keep, ffn1_send)
    dres1, ffn1, attn2, ffn2 = together((dres1, ffn1, add_up(attn2), add_up(ffn2)))
    ffn1 = scatter_stage(ffn1, 0, devices)
    for place in stages[1:-1]:
        attn2 = add_up(scatter_stage(attn2, place, devices))
    attn2 = scatter_stage(attn2, last, devices)
    ffn2 = gather_stage(ffn2, last, devices)
    grads_send, grads_mine, attn1_keep, attn1_send = run_attention_backward(
        0, scal, x, True, [dres1] + kept1[:4], dx2, attn_own, attn_other, tokens, slots, devices
    )
    attn1 = pair_sum(attn1_keep, attn1_send)
    attn1, ffn1, attn2, ffn2 = together((attn1, add_up(ffn1), add_up(attn2), ffn2))
    for place in reversed(stages[:-1]):
        ffn2 = gather_stage(ffn2, place, devices)
    for place in stages[1:]:
        ffn1 = add_up(scatter_stage(ffn1, place, devices))
    attn1 = add_up(scatter_stage(attn1, 0, devices))
    for place in stages[1:]:
        attn1 = add_up(scatter_stage(attn1, place, devices))
    for place in reversed(stages):
        ffn1 = gather_stage(ffn1, place, devices)
        attn2 = gather_stage(attn2, place, devices)
        attn1 = gather_stage(attn1, place, devices)
    grads_got = lax.ppermute(grads_send, "section", SWAP)
    is_first = scal[0] == 0

    def finish(first_sum, second_sum, shapes, smalls):
        lacking = jnp.where(is_first, second_sum, first_sum)
        got = lax.ppermute(lacking, "section", SWAP)
        results = [((1,) + shape, full) for shape in shapes] + [((1, n), full) for n in smalls]
        return single_step(
            functools.partial(unpack_kernel, shapes, smalls),
            scal,
            [first_sum, second_sum, got],
            results,
        )

    down_grad, up_grad, up_b, down_b, gain2, shift2 = finish(
        ffn1,
        ffn2,
        [(hidden_width, width), (width, hidden_width)],
        [hidden_width, width, width, width],
    )
    qkv_grad, out_grad, qv_b, out_b, gain1, shift1 = finish(
        attn1, attn2, [(width, 3 * width), (width, width)], [2 * width, width, width, width]
    )
    layer_outs = fill_other_half(scal, outs_mine, outs_got, 4)
    layer_in_grads = fill_other_half(scal, grads_mine, grads_got, 4)
    shape = (1, local_rows, slots, width)
    return (
        layer_outs.reshape(shape),
        layer_in_grads.reshape(shape),
        gain1,
        shift1,
        qkv_grad,
        qv_b,
        out_grad,
        out_b,
        gain2,
        shift2,
        up_grad,
        up_b,
        down_grad,
        down_b,
    )


def solution(mesh):
    in_specs = (
        P("dp", None, None),
        P("dp", None, None),
        P("dp", None),
        P("dp", None),
        P("section", None),
        P("section", None),
        P("section", None, None),
        P("section", None),
        P("section", None, None),
        P("section", None),
        P("section", None),
        P("section", None),
        P("section", None, None),
        P("section", None),
        P("section", None, None),
        P("section", None),
    )
    out_specs = (
        P("section", "dp", None, None),
        P("section", "dp", None, None),
        P("section", None),
        P("section", None),
        P("section", None, None),
        P("section", None),
        P("section", None, None),
        P("section", None),
        P("section", None),
        P("section", None),
        P("section", None, None),
        P("section", None),
        P("section", None, None),
        P("section", None),
    )
    return jax.shard_map(
        per_device, mesh=mesh, in_specs=in_specs, out_specs=out_specs, check_vma=False
    )
```

```python
import functools

import jax
import jax.numpy as jnp
from jax import lax
from jax.experimental import pallas as pl
from jax.experimental.pallas import tpu as pltpu
from jax.sharding import PartitionSpec as P

H = 6
R_F, R_FB, R_AB = 2, 2, 2
BLOCK = 128
norm_eps = 1e-06
forbidden = -1e30
sqrt_half = 0.7071067811865476
inverse_root_two_pi = 0.3989422804014327
VMEM_LIMIT = 60 * 1024 * 1024
low = jnp.bfloat16
full = jnp.float32


def nn(a, b):
    return lax.dot_general(a, b, (((1,), (0,)), ((), ())), preferred_element_type=full)


def nt(a, b):
    return lax.dot_general(a, b, (((1,), (1,)), ((), ())), preferred_element_type=full)


def tn(a, b):
    return lax.dot_general(a, b, (((0,), (0,)), ((), ())), preferred_element_type=full)


def column_blocks(width, step):
    return [(start, min(start + step, width)) for start in range(0, width, step)]


def fold_rows(values):
    return jnp.sum(values.reshape(values.shape[0] // 8, 8, values.shape[1]), axis=0)


def gelu_parts(hidden):
    size = jnp.abs(hidden)
    t = pl.reciprocal(1.0 + (0.3275911 * sqrt_half) * size, approx=True)
    bell = jnp.exp(-0.5 * (hidden * hidden))
    series = t * (
        0.127414796
        + t * (-0.142248368 + t * (0.7107068705 + t * (-0.7265760135 + t * 0.5307027145)))
    )
    tail = series * bell
    cdf = jnp.where(hidden >= 0.0, 1.0 - tail, tail)
    return (hidden * cdf, cdf + (hidden * inverse_root_two_pi) * bell)


def norm_parts(values):
    average = jnp.mean(values, axis=-1, keepdims=True)
    centred = values - average
    inverse = lax.rsqrt(jnp.mean(centred * centred, axis=-1, keepdims=True) + norm_eps)
    return (centred * inverse, inverse)


def head_lanes():
    lane = lax.broadcasted_iota(jnp.int32, (1, BLOCK), 1)
    first = jnp.where(lane < BLOCK // 2, 1.0, 0.0)
    return (first.astype(low), (1.0 - first).astype(low))


def fetch_weights(scal_ref, layer, own, other, held, sems):
    @pl.when(pl.program_id(0) == 0)
    def _():
        @pl.when(scal_ref[0] == layer)
        def _():
            for i in range(len(own)):
                pltpu.make_async_copy(own[i], held[i], sems.at[i]).start()

        @pl.when(scal_ref[0] != layer)
        def _():
            for i in range(len(own)):
                pltpu.make_async_copy(other[i], held[i], sems.at[i]).start()

        for i in range(len(own)):
            pltpu.make_async_copy(own[i], held[i], sems.at[i]).wait()


def row_index(scal_ref, steps_rows, r):
    return (scal_ref[0] * pl.num_programs(0) + pl.program_id(0)) * steps_rows + r


def pack_kernel(g1, b1, qv, ob, g2, b2, ub, db, out_ref):
    width = g1.shape[1]
    rows = [g1[...], b1[...], qv[:, :width], qv[:, width:], ob[...], g2[...], b2[...], db[...]]
    rows += [ub[:, c : c + width] for c in range(0, ub.shape[1], width)]
    out_ref[...] = jnp.concatenate(rows, axis=0)


def forward_kernel(layer, slots, scal_ref, x_ref, seg_ref, pad_ref, *rest):
    own, other = rest[0:5], rest[5:10]
    rest = rest[10:]
    if layer == 0:
        out_ref, rest = rest[0], rest[1:]
    else:
        send_ref, mine_ref, rest = rest[0], rest[1], rest[2:]
    qkv_ref, e_ref, rinv_ref, mixed_ref, xhat_ref, inv_ref, act_ref, slope_ref = rest[:8]
    wqkv, wout, wup, wdown, vec, na_s, res_s, nb_s, sg_s, bk_s, va_s, sems = rest[8:]
    fetch_weights(scal_ref, layer, own, other, (wqkv, wout, wup, wdown, vec), sems)
    tokens, width = x_ref.shape
    hidden_width = wup.shape[1]
    step = 64
    gain_a, shift_a = vec[0:1, :], vec[1:2, :]
    q_off, v_off = vec[2:3, :], vec[3:4, :]
    out_off, gain_b, shift_b, down_off = (vec[i : i + 1, :] for i in range(4, 8))
    for t in range(0, tokens, step):
        scaled, _ = norm_parts(x_ref[t : t + step, :].astype(full))
        na_s[t : t + step, :] = (scaled * gain_a + shift_a).astype(low)
    code = lax.broadcasted_iota(jnp.int32, (BLOCK, slots), 0)
    for r in range(tokens // slots):
        rows = slice(r * slots, (r + 1) * slots)
        row = row_index(scal_ref, tokens // slots, r)
        same = seg_ref[pl.ds(row, 1), :] == code
        pad = pad_ref[pl.ds(row, 1), :]
        sg_s[rows, :] = jnp.where(same, 1.0, 0.0).T.astype(low)
        bk_s[rows, :] = jnp.where(same & (pad > 0), 0.0, forbidden).T.astype(low)
        va_s[rows, :] = jnp.broadcast_to(pad.astype(full), (BLOCK, slots)).T
    for n0, n1 in column_blocks(3 * width, 512):
        part = nn(na_s[...], wqkv[:, n0:n1])
        for c in range(n0, n1, BLOCK):
            piece = part[:, c - n0 : c - n0 + BLOCK]
            if c < width:
                piece = (piece + q_off[:, c : c + BLOCK]) * 0.125
            elif c >= 2 * width:
                piece = piece + v_off[:, c - 2 * width : c - 2 * width + BLOCK]
            qkv_ref[:, c : c + BLOCK] = piece.astype(low)
    lanes = head_lanes()
    ones = jnp.ones((slots, BLOCK), low)
    for r in range(tokens // slots):
        rows = slice(r * slots, (r + 1) * slots)
        for p in range(H // 2):
            q2 = qkv_ref[rows, p * BLOCK : (p + 1) * BLOCK]
            k2 = qkv_ref[rows, width + p * BLOCK : width + (p + 1) * BLOCK]
            v2 = qkv_ref[rows, 2 * width + p * BLOCK : 2 * width + (p + 1) * BLOCK]
            keys = jnp.concatenate([k2, bk_s[rows, :]], axis=1)
            weights = []
            for i in range(2):
                queries = jnp.concatenate([q2 * lanes[i], sg_s[rows, :]], axis=1)
                scores = nt(queries, keys)
                e = jnp.exp(scores - jnp.max(scores, axis=1, keepdims=True)).astype(low)
                e_ref[rows, (2 * p + i) * slots : (2 * p + i + 1) * slots] = e
                weights.append(e)
            values = jnp.concatenate(
                [
                    jnp.concatenate([v2 * lanes[0], ones * lanes[0]], axis=1),
                    jnp.concatenate([v2 * lanes[1], ones * lanes[1]], axis=1),
                ],
                axis=0,
            )
            both = nn(jnp.concatenate(weights, axis=1), values)
            rinv = 1.0 / both[:, BLOCK:]
            rinv_ref[rows, p * BLOCK : (p + 1) * BLOCK] = rinv
            mixed_ref[rows, p * BLOCK : (p + 1) * BLOCK] = (both[:, :BLOCK] * rinv).astype(low)
    res_s[...] = x_ref[...].astype(full) + (nn(mixed_ref[...], wout[...]) + out_off)
    for t in range(0, tokens, step):
        scaled, inverse = norm_parts(res_s[t : t + step, :])
        xhat_ref[t : t + step, :] = scaled.astype(low)
        inv_ref[t : t + step, :] = jnp.broadcast_to(inverse, (step, BLOCK))
        nb_s[t : t + step, :] = (scaled * gain_b + shift_b).astype(low)
    for n0, n1 in column_blocks(hidden_width, 256):
        offset = jnp.concatenate(
            [
                vec[8 + c // width : 9 + c // width, c % width : c % width + BLOCK]
                for c in range(n0, n1, BLOCK)
            ],
            axis=1,
        )
        hidden = nn(nb_s[...], wup[:, n0:n1]) + offset
        if layer == 0:
            act, slope = gelu_parts(hidden)
        else:
            cdf = 0.5 * (1.0 + lax.erf(hidden * sqrt_half))
            bell = jnp.exp(-0.5 * (hidden * hidden))
            act, slope = hidden * cdf, cdf + (hidden * inverse_root_two_pi) * bell
        act_ref[:, n0:n1] = act.astype(low)
        slope_ref[:, n0:n1] = slope.astype(low)
    outcome = res_s[...] + (nn(act_ref[...], wdown[...]) + down_off)
    for c in range(0, width, BLOCK):
        piece = (va_s[...] * outcome[:, c : c + BLOCK]).astype(low)
        if layer == 0:
            out_ref[:, c : c + BLOCK] = piece
        else:
            before = x_ref[:, c : c + BLOCK]

            @pl.when(scal_ref[0] == 0)
            def _():
                send_ref[:, c : c + BLOCK] = piece
                mine_ref[:, c : c + BLOCK] = before

            @pl.when(scal_ref[0] != 0)
            def _():
                send_ref[:, c : c + BLOCK] = before
                mine_ref[:, c : c + BLOCK] = piece


def small_block(vectors):
    row = jnp.concatenate([jnp.sum(v, axis=0, keepdims=True) for v in vectors], axis=1)
    count = row.shape[1] // BLOCK
    pieces = [row[:, j * BLOCK : (j + 1) * BLOCK] for j in range(count)]
    padded = -(-count // 16) * 16
    if padded > count:
        pieces.append(jnp.zeros((padded - count, BLOCK), full))
    return jnp.concatenate(pieces, axis=0).astype(low)


def store_payload(scal_ref, keep_ref, send_ref, write):
    for h in range(2):

        @pl.when(scal_ref[0] == h)
        def _():
            write(keep_ref, h)

        @pl.when(scal_ref[0] != h)
        def _():
            write(send_ref, h)


def store_columns(ref, base, matrix, row0, rows):
    for b in range(matrix.shape[1] // BLOCK):
        ref[base + b * rows : base + (b + 1) * rows, :] = matrix[
            row0 : row0 + rows, b * BLOCK : (b + 1) * BLOCK
        ].astype(low)
    return base + rows * (matrix.shape[1] // BLOCK)


def store_rest(ref, base, block):
    ref[base : base + block.shape[0], :] = block
    base += block.shape[0]
    if base < ref.shape[0]:
        ref[base:, :] = jnp.zeros((ref.shape[0] - base, BLOCK), low)


def ffn_backward_kernel(
    layer, slots, scal_ref, dy_ref, xhat_ref, inv_ref, act_ref, slope_ref, pad_ref, *rest
):
    own, other = rest[0:3], rest[3:6]
    dres_ref, keep_ref, send_ref = rest[6:9]
    wup, wdown, vec, dd_s, ddt_s, nbt_s, dh_s, dnb_s, accd, accu, su, sd, sg, sb, sems = rest[9:]
    fetch_weights(scal_ref, layer, own, other, (wup, wdown, vec), sems)
    tokens, width = dy_ref.shape
    hidden_width = wup.shape[1]
    step = 64

    @pl.when(pl.program_id(0) == 0)
    def _():
        for ref in (accd, accu, su, sd, sg, sb):
            ref[...] = jnp.zeros_like(ref)

    gain_b, shift_b = vec[5:6, :], vec[6:7, :]
    for r in range(tokens // slots):
        rows = slice(r * slots, (r + 1) * slots)
        row = row_index(scal_ref, tokens // slots, r)
        pad = pad_ref[pl.ds(row, 1), :].astype(full)
        valid = jnp.broadcast_to(pad, (BLOCK, slots)).T.astype(low)
        for c in range(0, width, BLOCK):
            dd_s[rows, c : c + BLOCK] = dy_ref[rows, c : c + BLOCK] * valid
    ddt_s[...] = dd_s[...].T
    sd[...] += fold_rows(dd_s[...].astype(full))
    nbt_s[...] = (xhat_ref[...].astype(full) * gain_b + shift_b).astype(low).T
    for n0, n1 in column_blocks(hidden_width, 512 if layer else 256):
        back = nt(dd_s[...], wdown[n0:n1, :])
        dh = (back * slope_ref[:, n0:n1].astype(full)).astype(low)
        dh_s[:, n0:n1] = dh
        su[:, n0:n1] += fold_rows(dh.astype(full))
        accd[:, n0:n1] += nn(ddt_s[...], act_ref[:, n0:n1])
        accu[:, n0:n1] += nn(nbt_s[...], dh)
    dnb_s[...] = nt(dh_s[...], wup[...])
    for t in range(0, tokens, step):
        scaled = xhat_ref[t : t + step, :].astype(full)
        inverse = inv_ref[t : t + step, :]
        inverse = jnp.concatenate([inverse] * (width // BLOCK), axis=1)
        dn = dnb_s[t : t + step, :]
        sg[...] += fold_rows(dn * scaled)
        sb[...] += fold_rows(dn)
        e = dn * gain_b
        inner = (e - jnp.mean(e, axis=-1, keepdims=True)) - scaled * jnp.mean(
            e * scaled, axis=-1, keepdims=True
        )
        dres_ref[t : t + step, :] = dd_s[t : t + step, :].astype(full) + inverse * inner

    @pl.when(pl.program_id(0) == pl.num_programs(0) - 1)
    def _():
        small = small_block([su[...], sd[...], sg[...], sb[...]])

        def write(ref, h):
            half = hidden_width // 2
            for b in range(width // BLOCK):
                turned = accd[b * BLOCK : (b + 1) * BLOCK, h * half : (h + 1) * half].T
                ref[b * half : (b + 1) * half, :] = turned.astype(low)
            base = store_columns(ref, half * (width // BLOCK), accu, h * width // 2, width // 2)
            store_rest(ref, base, small)

        store_payload(scal_ref, keep_ref, send_ref, write)


def attention_backward_kernel(
    layer, slots, scal_ref, x_ref, dres_ref, qkv_ref, e_ref, rinv_ref, mixed_ref, *rest
):
    if layer == 0:
        later_ref, rest = rest[0], rest[1:]
    own, other, rest = rest[0:3], rest[3:6], rest[6:]
    if layer == 0:
        dsend_ref, dmine_ref, rest = rest[0], rest[1], rest[2:]
    else:
        dx_ref, rest = rest[0], rest[1:]
    keep_ref, send_ref = rest[0:2]
    wqkv, wout, vec, db_s, mixt_s, do_s, pr_s, dp_s, xh_s, iv_s, nat_s, dna_s = rest[2:14]
    accq, acco, sq, so, sg, sb, sems = rest[14:]
    fetch_weights(scal_ref, layer, own, other, (wqkv, wout, vec), sems)
    tokens, width = x_ref.shape
    step = 64

    @pl.when(pl.program_id(0) == 0)
    def _():
        for ref in (accq, acco, sq, so, sg, sb):
            ref[...] = jnp.zeros_like(ref)

    gain_a, shift_a = vec[0:1, :], vec[1:2, :]
    db_s[...] = dres_ref[...].astype(low)
    so[...] += fold_rows(db_s[...].astype(full))
    mixt_s[...] = mixed_ref[...].T
    acco[...] += nn(mixt_s[...], db_s[...])
    scaled_do = nt(db_s[...], wout[...]) * rinv_ref[...]
    do_s[...] = scaled_do.astype(low)
    pr_s[...] = (scaled_do * (-mixed_ref[...].astype(full))).astype(low)
    for t in range(0, tokens, step):
        scaled, inverse = norm_parts(x_ref[t : t + step, :].astype(full))
        xh_s[t : t + step, :] = scaled
        iv_s[t : t + step, :] = jnp.broadcast_to(inverse, (step, BLOCK))
        dna_s[t : t + step, :] = scaled * gain_a + shift_a
    nat_s[...] = dna_s[...].astype(low).T
    lanes = head_lanes()
    ones = jnp.ones((slots, BLOCK), low)
    for r in range(tokens // slots):
        rows = slice(r * slots, (r + 1) * slots)
        for p in range(H // 2):
            cols = slice(p * BLOCK, (p + 1) * BLOCK)
            q2 = qkv_ref[rows, p * BLOCK : (p + 1) * BLOCK]
            k2 = qkv_ref[rows, width + p * BLOCK : width + (p + 1) * BLOCK]
            v2 = qkv_ref[rows, 2 * width + p * BLOCK : 2 * width + (p + 1) * BLOCK]
            do2, pr2 = do_s[rows, cols], pr_s[rows, cols]
            values = jnp.concatenate([v2, ones], axis=1)
            weights, slopes, dos, qs, ks = [], [], [], [], []
            for i in range(2):
                e = e_ref[rows, (2 * p + i) * slots : (2 * p + i + 1) * slots]
                do = do2 * lanes[i]
                inner = nt(jnp.concatenate([do, pr2 * lanes[i]], axis=1), values)
                slopes.append((e.astype(full) * inner).astype(low))
                weights.append(e)
                dos.append(do)
                qs.append(q2 * lanes[i])
                ks.append(k2 * lanes[i])
            dv = tn(jnp.concatenate(weights, axis=0), jnp.concatenate(dos, axis=0))
            dk = tn(jnp.concatenate(slopes, axis=0), jnp.concatenate(qs, axis=0))
            dq = nn(jnp.concatenate(slopes, axis=1), jnp.concatenate(ks, axis=0)) * 0.125
            dp_s[rows, p * BLOCK : (p + 1) * BLOCK] = dq.astype(low)
            dp_s[rows, width + p * BLOCK : width + (p + 1) * BLOCK] = dk.astype(low)
            dp_s[rows, 2 * width + p * BLOCK : 2 * width + (p + 1) * BLOCK] = dv.astype(low)
    sq[:, :width] += fold_rows(dp_s[:, :width].astype(full))
    sq[:, width:] += fold_rows(dp_s[:, 2 * width :].astype(full))
    for n0, n1 in column_blocks(3 * width, 512):
        accq[:, n0:n1] += nn(nat_s[...], dp_s[:, n0:n1])
    dna_s[...] = nt(dp_s[...], wqkv[...])
    for t in range(0, tokens, step):
        part = slice(t, t + step)
        scaled = xh_s[part, :]
        inverse = iv_s[part, :]
        inverse = jnp.concatenate([inverse] * (width // BLOCK), axis=1)
        dn = dna_s[part, :]
        sg[...] += fold_rows(dn * scaled)
        sb[...] += fold_rows(dn)
        e = dn * gain_a
        inner = (e - jnp.mean(e, axis=-1, keepdims=True)) - scaled * jnp.mean(
            e * scaled, axis=-1, keepdims=True
        )
        dna_s[part, :] = dres_ref[part, :] + inverse * inner
    if layer == 0:

        @pl.when(scal_ref[0] == 0)
        def _():
            dmine_ref[...] = dna_s[...]
            dsend_ref[...] = later_ref[...]

        @pl.when(scal_ref[0] != 0)
        def _():
            dmine_ref[...] = later_ref[...].astype(full)
            dsend_ref[...] = dna_s[...].astype(low)

    else:
        dx_ref[...] = dna_s[...].astype(low)

    @pl.when(pl.program_id(0) == pl.num_programs(0) - 1)
    def _():
        small = small_block([sq[...], so[...], sg[...], sb[...]])

        def write(ref, h):
            base = store_columns(ref, 0, accq, h * width // 2, width // 2)
            base = store_columns(ref, base, acco, h * width // 2, width // 2)
            store_rest(ref, base, small)

        store_payload(scal_ref, keep_ref, send_ref, write)


def call_kernel(
    kernel, scal, steps, blocked, fixed, hbm, outs, fixed_outs, scratch, flops, moved, fuse=False
):
    own_index = lambda i, s: (i, 0)
    shared_index = lambda i, s: (s[0] * steps + i, 0)

    def spec(shape, shared):
        rows = shape[0] // (2 * steps if shared else steps)
        return pl.BlockSpec((rows, shape[1]), shared_index if shared else own_index)

    in_specs, args = [], []
    for array, shared in blocked:
        in_specs.append(spec(array.shape, shared))
        args.append(array)
    for array in fixed:
        in_specs.append(pl.BlockSpec(array.shape, lambda i, s, n=array.ndim: (0,) * n))
        args.append(array)
    for array in hbm:
        in_specs.append(pl.BlockSpec(memory_space=pl.ANY))
        args.append(array)
    out_specs, out_shapes = [], []
    for shape, dtype, shared in outs:
        out_specs.append(spec(shape, shared))
        out_shapes.append(jax.ShapeDtypeStruct(shape, dtype))
    for shape, dtype in fixed_outs:
        out_specs.append(pl.BlockSpec(shape, lambda i, s, n=len(shape): (0,) * n))
        out_shapes.append(jax.ShapeDtypeStruct(shape, dtype))
    return pl.pallas_call(
        kernel,
        grid_spec=pltpu.PrefetchScalarGridSpec(
            num_scalar_prefetch=1,
            grid=(steps,),
            in_specs=in_specs,
            out_specs=out_specs,
            scratch_shapes=scratch,
        ),
        out_shape=out_shapes,
        compiler_params=pltpu.CompilerParams(
            vmem_limit_bytes=VMEM_LIMIT, fuse_transposed_lhs_in_matmul=fuse
        ),
        cost_estimate=pl.CostEstimate(flops=flops, bytes_accessed=moved, transcendentals=0),
    )(scal, *args)


def run_forward(layer, scal, x, shared, segments, pad, own, other, tokens, slots):
    width = x.shape[1]
    hidden_width = own[2].shape[1]
    steps = tokens // (R_F * slots)
    per_step = R_F * slots
    if layer == 0:
        outs = [((tokens, width), low, False)]
    else:
        outs = [((tokens, width), low, False), ((2 * tokens, width), low, True)]
    outs += [
        ((tokens, 3 * width), low, False),
        ((tokens, H * slots), low, False),
        ((tokens, width), full, False),
        ((tokens, width), low, False),
        ((tokens, width), low, False),
        ((tokens, BLOCK), full, False),
        ((tokens, hidden_width), low, False),
        ((tokens, hidden_width), low, False),
    ]
    scratch = [pltpu.VMEM(w.shape, w.dtype) for w in own] + [
        pltpu.VMEM((per_step, width), low),
        pltpu.VMEM((per_step, width), full),
        pltpu.VMEM((per_step, width), low),
        pltpu.VMEM((per_step, BLOCK), low),
        pltpu.VMEM((per_step, BLOCK), low),
        pltpu.VMEM((per_step, BLOCK), full),
        pltpu.SemaphoreType.DMA((5,)),
    ]
    return call_kernel(
        functools.partial(forward_kernel, layer, slots),
        scal,
        steps,
        [(x, shared)],
        [segments, pad],
        list(own) + list(other),
        outs,
        [],
        scratch,
        2 * tokens * (4 * width * width + 2 * width * hidden_width + 2 * slots * width),
        tokens * 14000,
    )


def payload_rows(used, devices):
    unit = devices * 16
    return -(-used // unit) * unit


def run_ffn_backward(layer, scal, dy, shared, pad, saved, own, other, tokens, slots, devices):
    width, hidden_width = own[0].shape
    steps = tokens // (R_FB * slots)
    per_step = R_FB * slots
    rows = payload_rows(hidden_width * width // BLOCK + 32, devices)
    scratch = [pltpu.VMEM(w.shape, w.dtype) for w in own] + [
        pltpu.VMEM((per_step, width), low),
        pltpu.VMEM((width, per_step), low),
        pltpu.VMEM((width, per_step), low),
        pltpu.VMEM((per_step, hidden_width), low),
        pltpu.VMEM((per_step, width), full),
        pltpu.VMEM((width, hidden_width), full),
        pltpu.VMEM((width, hidden_width), full),
        pltpu.VMEM((8, hidden_width), full),
        pltpu.VMEM((8, width), full),
        pltpu.VMEM((8, width), full),
        pltpu.VMEM((8, width), full),
        pltpu.SemaphoreType.DMA((3,)),
    ]
    return call_kernel(
        functools.partial(ffn_backward_kernel, layer, slots),
        scal,
        steps,
        [(dy, shared)] + [(array, False) for array in saved],
        [pad],
        list(own) + list(other),
        [((tokens, width), full, False)],
        [((rows, BLOCK), low), ((rows, BLOCK), low)],
        scratch,
        8 * tokens * width * hidden_width,
        tokens * 10000,
    )


def run_attention_backward(layer, scal, x, shared, saved, later, own, other, tokens, slots, devices):
    width = x.shape[1]
    steps = tokens // (R_AB * slots)
    per_step = R_AB * slots
    rows = payload_rows(2 * width * width // BLOCK + 16, devices)
    blocked = [(x, shared)] + [(array, False) for array in saved]
    if layer == 0:
        blocked.append((later, False))
        outs = [((tokens, width), low, False), ((2 * tokens, width), full, True)]
    else:
        outs = [((tokens, width), low, False)]
    scratch = [pltpu.VMEM(w.shape, w.dtype) for w in own] + [
        pltpu.VMEM((per_step, width), low),
        pltpu.VMEM((width, per_step), low),
        pltpu.VMEM((per_step, width), low),
        pltpu.VMEM((per_step, width), low),
        pltpu.VMEM((per_step, 3 * width), low),
        pltpu.VMEM((per_step, width), full),
        pltpu.VMEM((per_step, BLOCK), full),
        pltpu.VMEM((width, per_step), low),
        pltpu.VMEM((per_step, width), full),
        pltpu.VMEM((width, 3 * width), full),
        pltpu.VMEM((width, width), full),
        pltpu.VMEM((8, 2 * width), full),
        pltpu.VMEM((8, width), full),
        pltpu.VMEM((8, width), full),
        pltpu.VMEM((8, width), full),
        pltpu.SemaphoreType.DMA((3,)),
    ]
    return call_kernel(
        functools.partial(attention_backward_kernel, layer, slots),
        scal,
        steps,
        blocked,
        [],
        list(own) + list(other),
        outs,
        [((rows, BLOCK), low), ((rows, BLOCK), low)],
        scratch,
        2 * tokens * (8 * width * width + 5 * slots * width),
        tokens * 11000,
        fuse=layer == 1,
    )


def fill_kernel(scal_ref, got_ref, held_ref, out_ref):
    del scal_ref, held_ref
    out_ref[...] = got_ref[...].astype(out_ref.dtype)


def fill_other_half(scal, held, got, steps):
    rows = got.shape[0] // steps
    return pl.pallas_call(
        fill_kernel,
        grid_spec=pltpu.PrefetchScalarGridSpec(
            num_scalar_prefetch=1,
            grid=(steps,),
            in_specs=[
                pl.BlockSpec((rows, got.shape[1]), lambda i, s: (i, 0)),
                pl.BlockSpec(memory_space=pl.ANY),
            ],
            out_specs=pl.BlockSpec(
                (rows, got.shape[1]), lambda i, s: ((1 - s[0]) * steps + i, 0)
            ),
        ),
        out_shape=jax.ShapeDtypeStruct(held.shape, held.dtype),
        input_output_aliases={2: 0},
        cost_estimate=pl.CostEstimate(
            flops=0, bytes_accessed=8 * got.size, transcendentals=0
        ),
    )(scal, got, held)


def single_step(kernel, scal, arrays, shapes, scratch=()):
    whole = lambda shape: pl.BlockSpec(shape, lambda i, s, n=len(shape): (0,) * n)
    moved = sum(a.size * a.dtype.itemsize for a in arrays)
    return pl.pallas_call(
        kernel,
        grid_spec=pltpu.PrefetchScalarGridSpec(
            num_scalar_prefetch=1,
            grid=(1,),
            in_specs=[whole(a.shape) for a in arrays],
            out_specs=[whole(shape) for shape, _ in shapes],
            scratch_shapes=list(scratch),
        ),
        out_shape=[jax.ShapeDtypeStruct(shape, dtype) for shape, dtype in shapes],
        compiler_params=pltpu.CompilerParams(vmem_limit_bytes=VMEM_LIMIT),
        cost_estimate=pl.CostEstimate(flops=0, bytes_accessed=3 * moved, transcendentals=0),
    )(scal, *arrays)


def unpack_kernel(shapes, smalls, scal_ref, first, second, got, *refs):
    matrices, vectors = refs[: len(shapes)], refs[len(shapes) :]

    def write(source, h):
        base = 0
        for (rows, columns), out_ref in zip(shapes, matrices):
            half = rows // 2
            for b in range(columns // BLOCK):
                out_ref[0, h * half : (h + 1) * half, b * BLOCK : (b + 1) * BLOCK] = source[
                    base : base + half, :
                ].astype(full)
                base += half

    @pl.when(scal_ref[0] == 0)
    def _():
        write(first, 0)
        write(got, 1)

    @pl.when(scal_ref[0] != 0)
    def _():
        write(got, 0)
        write(second, 1)

    base = sum(rows // 2 * columns // BLOCK for rows, columns in shapes)
    padded = -(-sum(smalls) // BLOCK // 16) * 16
    block = got[base : base + padded, :].astype(full)
    row = 0
    for size, out_ref in zip(smalls, vectors):
        for c in range(0, size, BLOCK):
            out_ref[0:1, c : c + BLOCK] = block[row : row + 1, :]
            row += 1


SWAP = [(0, 1), (1, 0)]


def stage_sizes(devices):
    sizes = []
    while devices > 1:
        size = 4 if devices % 4 == 0 and devices != 8 else devices
        sizes.append(size)
        devices //= size
    return sizes


def stage_groups(place, devices):
    sizes = stage_sizes(devices)
    stride = 1
    for size in sizes[:place]:
        stride *= size
    size = sizes[place]
    groups = []
    for start in range(devices):
        if start // stride % size == 0:
            groups.append([start + k * stride for k in range(size)])
    return groups


def scatter_stage(array, place, devices):
    groups = stage_groups(place, devices)
    return lax.psum_scatter(
        array, "dp", scatter_dimension=0, axis_index_groups=groups, tiled=True
    )


def total_stage(array, place, devices):
    return lax.psum(array, "dp", axis_index_groups=stage_groups(place, devices))


def gather_stage(array, place, devices):
    groups = stage_groups(place, devices)
    return lax.all_gather(array, "dp", axis_index_groups=groups, tiled=True)


def pair_sum(keep, send):
    got = lax.ppermute(send, "section", SWAP)
    return (keep.astype(full) + got.astype(full)).astype(low)


together = lax.optimization_barrier


def per_device(
    activations,
    cotangent,
    segment_ids,
    pad_mask,
    norm1_gain,
    norm1_bias,
    qkv_weight,
    qv_bias,
    out_weight,
    out_bias,
    norm2_gain,
    norm2_bias,
    up_weight,
    up_bias,
    down_weight,
    down_bias,
):
    devices = lax.axis_size("dp")
    scal = lax.axis_index("section").astype(jnp.int32).reshape(1)
    local_rows, slots, width = activations.shape
    hidden_width = up_weight.shape[-1]
    tokens = local_rows // 2 * slots

    vec_rows = 8 + hidden_width // width
    vec = pl.pallas_call(
        pack_kernel, out_shape=jax.ShapeDtypeStruct((vec_rows, width), full)
    )(norm1_gain, norm1_bias, qv_bias, out_bias, norm2_gain, norm2_bias, up_bias, down_bias)
    own = (qkv_weight[0], out_weight[0], up_weight[0], down_weight[0], vec)
    other = tuple(lax.ppermute(w, "section", SWAP) for w in own)
    attn_own, attn_other = (own[0], own[1], own[4]), (other[0], other[1], other[4])
    ffn_own, ffn_other = own[2:], other[2:]

    x = activations.reshape(-1, width)
    seed = cotangent.reshape(-1, width)

    first, *kept1 = run_forward(
        0, scal, x, True, segment_ids, pad_mask, own, other, tokens, slots
    )
    outs_send, outs_mine, *kept2 = run_forward(
        1, scal, first, False, segment_ids, pad_mask, own, other, tokens, slots
    )
    outs_got = lax.ppermute(outs_send, "section", SWAP)

    dres2, ffn2_keep, ffn2_send = run_ffn_backward(
        1, scal, seed, True, pad_mask, kept2[4:], ffn_own, ffn_other, tokens, slots, devices
    )
    stages = list(range(len(stage_sizes(devices))))
    ffn2 = pair_sum(ffn2_keep, ffn2_send)
    dres2, ffn2 = together((dres2, ffn2))
    ffn2 = scatter_stage(ffn2, 0, devices)
    dx2, attn2_keep, attn2_send = run_attention_backward(
        1, scal, first, False, [dres2] + kept2[:4], None, attn_own, attn_other, tokens, slots, devices
    )
    attn2 = pair_sum(attn2_keep, attn2_send)
    dx2, attn2, ffn2 = together((dx2, attn2, ffn2))
    for place in stages[1:]:
        ffn2 = scatter_stage(ffn2, place, devices)
    attn2, ffn2 = together((attn2, ffn2))
    attn2 = scatter_stage(attn2, 0, devices)
    dres1, ffn1_keep, ffn1_send = run_ffn_backward(
        0, scal, dx2, False, pad_mask, kept1[4:], ffn_own, ffn_other, tokens, slots, devices
    )
    ffn1 = pair_sum(ffn1_keep, ffn1_send)
    dres1, ffn1, attn2, ffn2 = together((dres1, ffn1, attn2, ffn2))
    for place in stages[1:]:
        attn2 = total_stage(attn2, place, devices)
    for place in reversed(stages[1:]):
        ffn2 = gather_stage(ffn2, place, devices)
    attn2, ffn2, ffn1 = together((attn2, ffn2, ffn1))
    ffn1 = scatter_stage(ffn1, 0, devices)
    grads_send, grads_mine, attn1_keep, attn1_send = run_attention_backward(
        0, scal, x, True, [dres1] + kept1[:4], dx2, attn_own, attn_other, tokens, slots, devices
    )
    attn1 = pair_sum(attn1_keep, attn1_send)
    for place in stages[1:]:
        ffn1 = total_stage(ffn1, place, devices)
    ffn2, ffn1 = together((ffn2, ffn1))
    ffn2 = gather_stage(ffn2, 0, devices)
    attn1, ffn2 = together((attn1, ffn2))
    attn1 = scatter_stage(attn1, 0, devices)
    for place in stages[1:]:
        attn1 = total_stage(attn1, place, devices)
    attn2, attn1 = together((attn2, attn1))
    attn2 = gather_stage(attn2, 0, devices)
    ffn1, attn2 = together((ffn1, attn2))
    ffn1 = gather_stage(ffn1, 0, devices)
    attn1, ffn1 = together((attn1, ffn1))
    attn1 = gather_stage(attn1, 0, devices)
    grads_got = lax.ppermute(grads_send, "section", SWAP)
    is_first = scal[0] == 0

    def finish(first_sum, second_sum, shapes, smalls):
        lacking = jnp.where(is_first, second_sum, first_sum)
        got = lax.ppermute(lacking, "section", SWAP)
        results = [((1,) + shape, full) for shape in shapes] + [((1, n), full) for n in smalls]
        return single_step(
            functools.partial(unpack_kernel, shapes, smalls),
            scal,
            [first_sum, second_sum, got],
            results,
        )

    down_grad, up_grad, up_b, down_b, gain2, shift2 = finish(
        ffn1,
        ffn2,
        [(hidden_width, width), (width, hidden_width)],
        [hidden_width, width, width, width],
    )
    qkv_grad, out_grad, qv_b, out_b, gain1, shift1 = finish(
        attn1, attn2, [(width, 3 * width), (width, width)], [2 * width, width, width, width]
    )
    layer_outs = fill_other_half(scal, outs_mine, outs_got, 4)
    layer_in_grads = fill_other_half(scal, grads_mine, grads_got, 4)
    shape = (1, local_rows, slots, width)
    return (
        layer_outs.reshape(shape),
        layer_in_grads.reshape(shape),
        gain1,
        shift1,
        qkv_grad,
        qv_b,
        out_grad,
        out_b,
        gain2,
        shift2,
        up_grad,
        up_b,
        down_grad,
        down_b,
    )


def solution(mesh):
    in_specs = (
        P("dp", None, None),
        P("dp", None, None),
        P("dp", None),
        P("dp", None),
        P("section", None),
        P("section", None),
        P("section", None, None),
        P("section", None),
        P("section", None, None),
        P("section", None),
        P("section", None),
        P("section", None),
        P("section", None, None),
        P("section", None),
        P("section", None, None),
        P("section", None),
    )
    out_specs = (
        P("section", "dp", None, None),
        P("section", "dp", None, None),
        P("section", None),
        P("section", None),
        P("section", None, None),
        P("section", None),
        P("section", None, None),
        P("section", None),
        P("section", None),
        P("section", None),
        P("section", None, None),
        P("section", None),
        P("section", None, None),
        P("section", None),
    )
    return jax.shard_map(
        per_device, mesh=mesh, in_specs=in_specs, out_specs=out_specs, check_vma=False
    )
```

```python
import functools

import jax
import jax.numpy as jnp
from jax import lax
from jax.experimental import pallas as pl
from jax.experimental.pallas import tpu as pltpu
from jax.sharding import PartitionSpec as P

H = 6
R_F, R_FB, R_AB = 2, 2, 2
BLOCK = 128
norm_eps = 1e-06
forbidden = -1e30
sqrt_half = 0.7071067811865476
inverse_root_two_pi = 0.3989422804014327
VMEM_LIMIT = 60 * 1024 * 1024
low = jnp.bfloat16
full = jnp.float32


def nn(a, b):
    return lax.dot_general(a, b, (((1,), (0,)), ((), ())), preferred_element_type=full)


def nt(a, b):
    return lax.dot_general(a, b, (((1,), (1,)), ((), ())), preferred_element_type=full)


def tn(a, b):
    return lax.dot_general(a, b, (((0,), (0,)), ((), ())), preferred_element_type=full)


def column_blocks(width, step):
    return [(start, min(start + step, width)) for start in range(0, width, step)]


def fold_rows(values):
    return jnp.sum(values.reshape(values.shape[0] // 8, 8, values.shape[1]), axis=0)


def gelu_parts(hidden):
    cdf = 0.5 * (1.0 + lax.erf(hidden * sqrt_half))
    bell = jnp.exp(-0.5 * (hidden * hidden))
    return (hidden * cdf, cdf + (hidden * inverse_root_two_pi) * bell)


def norm_parts(values):
    average = jnp.mean(values, axis=-1, keepdims=True)
    centred = values - average
    inverse = lax.rsqrt(jnp.mean(centred * centred, axis=-1, keepdims=True) + norm_eps)
    return (centred * inverse, inverse)


def head_lanes():
    lane = lax.broadcasted_iota(jnp.int32, (1, BLOCK), 1)
    first = jnp.where(lane < BLOCK // 2, 1.0, 0.0)
    return (first.astype(low), (1.0 - first).astype(low))


def fetch_weights(scal_ref, layer, own, other, held, sems):
    @pl.when(pl.program_id(0) == 0)
    def _():
        @pl.when(scal_ref[0] == layer)
        def _():
            for i in range(len(own)):
                pltpu.make_async_copy(own[i], held[i], sems.at[i]).start()

        @pl.when(scal_ref[0] != layer)
        def _():
            for i in range(len(own)):
                pltpu.make_async_copy(other[i], held[i], sems.at[i]).start()

        for i in range(len(own)):
            pltpu.make_async_copy(own[i], held[i], sems.at[i]).wait()


def row_index(scal_ref, steps_rows, r):
    return (scal_ref[0] * pl.num_programs(0) + pl.program_id(0)) * steps_rows + r


def pack_kernel(g1, b1, qv, ob, g2, b2, ub, db, out_ref):
    width = g1.shape[1]
    rows = [g1[...], b1[...], qv[:, :width], qv[:, width:], ob[...], g2[...], b2[...], db[...]]
    rows += [ub[:, c : c + width] for c in range(0, ub.shape[1], width)]
    out_ref[...] = jnp.concatenate(rows, axis=0)


def forward_kernel(layer, slots, scal_ref, x_ref, seg_ref, pad_ref, *rest):
    own, other = rest[0:5], rest[5:10]
    rest = rest[10:]
    if layer == 0:
        out_ref, rest = rest[0], rest[1:]
    else:
        send_ref, mine_ref, rest = rest[0], rest[1], rest[2:]
    qkv_ref, e_ref, rinv_ref, mixed_ref, xhat_ref, inv_ref, act_ref, slope_ref = rest[:8]
    wqkv, wout, wup, wdown, vec, na_s, res_s, nb_s, sg_s, bk_s, va_s, sems = rest[8:]
    fetch_weights(scal_ref, layer, own, other, (wqkv, wout, wup, wdown, vec), sems)
    tokens, width = x_ref.shape
    hidden_width = wup.shape[1]
    step = 64
    gain_a, shift_a = vec[0:1, :], vec[1:2, :]
    q_off, v_off = vec[2:3, :], vec[3:4, :]
    out_off, gain_b, shift_b, down_off = (vec[i : i + 1, :] for i in range(4, 8))
    for t in range(0, tokens, step):
        scaled, _ = norm_parts(x_ref[t : t + step, :].astype(full))
        na_s[t : t + step, :] = (scaled * gain_a + shift_a).astype(low)
    code = lax.broadcasted_iota(jnp.int32, (BLOCK, slots), 0)
    for r in range(tokens // slots):
        rows = slice(r * slots, (r + 1) * slots)
        row = row_index(scal_ref, tokens // slots, r)
        same = seg_ref[pl.ds(row, 1), :] == code
        pad = pad_ref[pl.ds(row, 1), :]
        sg_s[rows, :] = jnp.where(same, 1.0, 0.0).T.astype(low)
        bk_s[rows, :] = jnp.where(same & (pad > 0), 0.0, forbidden).T.astype(low)
        va_s[rows, :] = jnp.broadcast_to(pad.astype(full), (BLOCK, slots)).T
    for n0, n1 in column_blocks(3 * width, 512):
        part = nn(na_s[...], wqkv[:, n0:n1])
        for c in range(n0, n1, BLOCK):
            piece = part[:, c - n0 : c - n0 + BLOCK]
            if c < width:
                piece = (piece + q_off[:, c : c + BLOCK]) * 0.125
            elif c >= 2 * width:
                piece = piece + v_off[:, c - 2 * width : c - 2 * width + BLOCK]
            qkv_ref[:, c : c + BLOCK] = piece.astype(low)
    lanes = head_lanes()
    ones = jnp.ones((slots, BLOCK), low)
    for r in range(tokens // slots):
        rows = slice(r * slots, (r + 1) * slots)
        for p in range(H // 2):
            q2 = qkv_ref[rows, p * BLOCK : (p + 1) * BLOCK]
            k2 = qkv_ref[rows, width + p * BLOCK : width + (p + 1) * BLOCK]
            v2 = qkv_ref[rows, 2 * width + p * BLOCK : 2 * width + (p + 1) * BLOCK]
            keys = jnp.concatenate([k2, bk_s[rows, :]], axis=1)
            weights = []
            for i in range(2):
                queries = jnp.concatenate([q2 * lanes[i], sg_s[rows, :]], axis=1)
                scores = nt(queries, keys)
                e = jnp.exp(scores - jnp.max(scores, axis=1, keepdims=True)).astype(low)
                e_ref[rows, (2 * p + i) * slots : (2 * p + i + 1) * slots] = e
                weights.append(e)
            values = jnp.concatenate(
                [
                    jnp.concatenate([v2 * lanes[0], ones * lanes[0]], axis=1),
                    jnp.concatenate([v2 * lanes[1], ones * lanes[1]], axis=1),
                ],
                axis=0,
            )
            both = nn(jnp.concatenate(weights, axis=1), values)
            rinv = 1.0 / both[:, BLOCK:]
            rinv_ref[rows, p * BLOCK : (p + 1) * BLOCK] = rinv
            mixed_ref[rows, p * BLOCK : (p + 1) * BLOCK] = (both[:, :BLOCK] * rinv).astype(low)
    res_s[...] = x_ref[...].astype(full) + (nn(mixed_ref[...], wout[...]) + out_off)
    for t in range(0, tokens, step):
        scaled, inverse = norm_parts(res_s[t : t + step, :])
        xhat_ref[t : t + step, :] = scaled.astype(low)
        inv_ref[t : t + step, :] = jnp.broadcast_to(inverse, (step, BLOCK))
        nb_s[t : t + step, :] = (scaled * gain_b + shift_b).astype(low)
    for n0, n1 in column_blocks(hidden_width, 256):
        offset = jnp.concatenate(
            [
                vec[8 + c // width : 9 + c // width, c % width : c % width + BLOCK]
                for c in range(n0, n1, BLOCK)
            ],
            axis=1,
        )
        hidden = nn(nb_s[...], wup[:, n0:n1]) + offset
        act, slope = gelu_parts(hidden)
        act_ref[:, n0:n1] = act.astype(low)
        slope_ref[:, n0:n1] = slope.astype(low)
    outcome = res_s[...] + (nn(act_ref[...], wdown[...]) + down_off)
    for c in range(0, width, BLOCK):
        piece = (va_s[...] * outcome[:, c : c + BLOCK]).astype(low)
        if layer == 0:
            out_ref[:, c : c + BLOCK] = piece
        else:
            before = x_ref[:, c : c + BLOCK]

            @pl.when(scal_ref[0] == 0)
            def _():
                send_ref[:, c : c + BLOCK] = piece
                mine_ref[:, c : c + BLOCK] = before

            @pl.when(scal_ref[0] != 0)
            def _():
                send_ref[:, c : c + BLOCK] = before
                mine_ref[:, c : c + BLOCK] = piece


def small_block(vectors):
    row = jnp.concatenate([jnp.sum(v, axis=0, keepdims=True) for v in vectors], axis=1)
    count = row.shape[1] // BLOCK
    pieces = [row[:, j * BLOCK : (j + 1) * BLOCK] for j in range(count)]
    padded = -(-count // 16) * 16
    if padded > count:
        pieces.append(jnp.zeros((padded - count, BLOCK), full))
    return jnp.concatenate(pieces, axis=0).astype(low)


def store_payload(scal_ref, keep_ref, send_ref, write):
    for h in range(2):

        @pl.when(scal_ref[0] == h)
        def _():
            write(keep_ref, h)

        @pl.when(scal_ref[0] != h)
        def _():
            write(send_ref, h)


def store_columns(ref, base, matrix, row0, rows):
    for b in range(matrix.shape[1] // BLOCK):
        ref[base + b * rows : base + (b + 1) * rows, :] = matrix[
            row0 : row0 + rows, b * BLOCK : (b + 1) * BLOCK
        ].astype(low)
    return base + rows * (matrix.shape[1] // BLOCK)


def store_rest(ref, base, block):
    ref[base : base + block.shape[0], :] = block
    base += block.shape[0]
    if base < ref.shape[0]:
        ref[base:, :] = jnp.zeros((ref.shape[0] - base, BLOCK), low)


def norm_backward(dn, gain, scaled, inverse):
    e = dn * gain
    inner = (e - jnp.mean(e, axis=-1, keepdims=True)) - scaled * jnp.mean(
        e * scaled, axis=-1, keepdims=True
    )
    return jnp.concatenate([inverse] * (dn.shape[1] // BLOCK), axis=1) * inner


def ffn_backward_kernel(
    layer, slots, scal_ref, dy_ref, mixed_ref, xhat_ref, inv_ref, act_ref, slope_ref, pad_ref, *rest
):
    own, other = rest[0:3], rest[3:6]
    dres_ref, keep_ref, send_ref = rest[6:9]
    wup, wdown, vec, dd_s, ddt_s, nbt_s, mixt_s, dh_s, dnb_s = rest[9:18]
    accd, accu, acco, su, sd, so, sems = rest[18:]
    fetch_weights(scal_ref, layer, own, other, (wup, wdown, vec), sems)
    tokens, width = dy_ref.shape
    hidden_width = wup.shape[1]
    step = 64

    @pl.when(pl.program_id(0) == 0)
    def _():
        for ref in (accd, accu, acco, su, sd, so):
            ref[...] = jnp.zeros_like(ref)

    gain_b = vec[5:6, :]
    for r in range(tokens // slots):
        rows = slice(r * slots, (r + 1) * slots)
        row = row_index(scal_ref, tokens // slots, r)
        pad = pad_ref[pl.ds(row, 1), :].astype(full)
        valid = jnp.broadcast_to(pad, (BLOCK, slots)).T.astype(low)
        for c in range(0, width, BLOCK):
            dd_s[rows, c : c + BLOCK] = dy_ref[rows, c : c + BLOCK] * valid
    ddt_s[...] = dd_s[...].T
    sd[...] += fold_rows(dd_s[...].astype(full))
    nbt_s[...] = xhat_ref[...].T
    mixt_s[...] = mixed_ref[...].T
    for n0, n1 in column_blocks(hidden_width, 512):
        back = nt(dd_s[...], wdown[n0:n1, :])
        dh = (back * slope_ref[:, n0:n1].astype(full)).astype(low)
        dh_s[:, n0:n1] = dh
        su[:, n0:n1] += fold_rows(dh.astype(full))
        accd[:, n0:n1] += nn(ddt_s[...], act_ref[:, n0:n1])
        accu[:, n0:n1] += nn(nbt_s[...], dh)
    dnb_s[...] = nt(dh_s[...], wup[...])
    for t in range(0, tokens, step):
        part = slice(t, t + step)
        change = norm_backward(
            dnb_s[part, :], gain_b, xhat_ref[part, :].astype(full), inv_ref[part, :]
        )
        dres = dd_s[part, :].astype(full) + change
        dres_ref[part, :] = dres
        dd_s[part, :] = dres.astype(low)
    so[...] += fold_rows(dd_s[...].astype(full))
    acco[...] += nn(mixt_s[...], dd_s[...])

    @pl.when(pl.program_id(0) == pl.num_programs(0) - 1)
    def _():
        small = small_block([su[...], sd[...], so[...]])

        def write(ref, h):
            half = hidden_width // 2
            for b in range(width // BLOCK):
                turned = accd[b * BLOCK : (b + 1) * BLOCK, h * half : (h + 1) * half].T
                ref[b * half : (b + 1) * half, :] = turned.astype(low)
            base = store_columns(ref, half * (width // BLOCK), accu, h * width // 2, width // 2)
            base = store_columns(ref, base, acco, h * width // 2, width // 2)
            store_rest(ref, base, small)

        store_payload(scal_ref, keep_ref, send_ref, write)


def input_gradient(scal_ref, layer, x_ref, dres_ref, dp_ref, wqkv, vec, later_ref, outs, dna_s):
    tokens, width = x_ref.shape
    step = 64
    dna_s[...] = nt(dp_ref[...], wqkv[...])
    for t in range(0, tokens, step):
        part = slice(t, t + step)
        scaled, inverse = norm_parts(x_ref[part, :].astype(full))
        inverse = jnp.broadcast_to(inverse, (step, BLOCK))
        change = norm_backward(dna_s[part, :], vec[0:1, :], scaled, inverse)
        dna_s[part, :] = dres_ref[part, :] + change
    if layer == 0:
        dsend_ref, dmine_ref = outs

        @pl.when(scal_ref[0] == 0)
        def _():
            dmine_ref[...] = dna_s[...]
            dsend_ref[...] = later_ref[...]

        @pl.when(scal_ref[0] != 0)
        def _():
            dmine_ref[...] = later_ref[...].astype(full)
            dsend_ref[...] = dna_s[...].astype(low)

    else:
        outs[0][...] = dna_s[...].astype(low)


def input_gradient_kernel(layer, scal_ref, x_ref, dres_ref, dp_ref, later_ref, *rest):
    own, other = rest[0:2], rest[2:4]
    outs = rest[4:6]
    wqkv, vec, dna_s, sems = rest[6:]
    fetch_weights(scal_ref, layer, own, other, (wqkv, vec), sems)
    input_gradient(scal_ref, layer, x_ref, dres_ref, dp_ref, wqkv, vec, later_ref, outs, dna_s)


def attention_backward_kernel(
    layer, slots, scal_ref, x_ref, dres_ref, qkv_ref, e_ref, rinv_ref, mixed_ref, *rest
):
    own, other, rest = rest[0:3], rest[3:6], rest[6:]
    result_ref, keep_ref, send_ref, rest = rest[0], rest[1], rest[2], rest[3:]
    wqkv, wout, vec, db_s, do_s, pr_s, xt_s, dna_s = rest[:8]
    if layer == 0:
        dp_s, rest = result_ref, rest[8:]
    else:
        dp_s, rest = rest[8], rest[9:]
    accq, sq, sems = rest
    fetch_weights(scal_ref, layer, own, other, (wqkv, wout, vec), sems)
    tokens, width = x_ref.shape
    step = 64

    @pl.when(pl.program_id(0) == 0)
    def _():
        for ref in (accq, sq):
            ref[...] = jnp.zeros_like(ref)

    db_s[...] = dres_ref[...].astype(low)
    scaled_do = nt(db_s[...], wout[...]) * rinv_ref[...]
    do_s[...] = scaled_do.astype(low)
    pr_s[...] = (scaled_do * (-mixed_ref[...].astype(full))).astype(low)
    for t in range(0, tokens, step):
        scaled, _ = norm_parts(x_ref[t : t + step, :].astype(full))
        db_s[t : t + step, :] = scaled.astype(low)
    xt_s[...] = db_s[...].T
    lanes = head_lanes()
    ones = jnp.ones((slots, BLOCK), low)
    for r in range(tokens // slots):
        rows = slice(r * slots, (r + 1) * slots)
        for p in range(H // 2):
            cols = slice(p * BLOCK, (p + 1) * BLOCK)
            q2 = qkv_ref[rows, p * BLOCK : (p + 1) * BLOCK]
            k2 = qkv_ref[rows, width + p * BLOCK : width + (p + 1) * BLOCK]
            v2 = qkv_ref[rows, 2 * width + p * BLOCK : 2 * width + (p + 1) * BLOCK]
            do2, pr2 = do_s[rows, cols], pr_s[rows, cols]
            values = jnp.concatenate([v2, ones], axis=1)
            weights, slopes, dos, qs, ks = [], [], [], [], []
            for i in range(2):
                e = e_ref[rows, (2 * p + i) * slots : (2 * p + i + 1) * slots]
                do = do2 * lanes[i]
                inner = nt(jnp.concatenate([do, pr2 * lanes[i]], axis=1), values)
                slopes.append((e.astype(full) * inner).astype(low))
                weights.append(e)
                dos.append(do)
                qs.append(q2 * lanes[i])
                ks.append(k2 * lanes[i])
            dv = tn(jnp.concatenate(weights, axis=0), jnp.concatenate(dos, axis=0))
            dk = tn(jnp.concatenate(slopes, axis=0), jnp.concatenate(qs, axis=0))
            dq = nn(jnp.concatenate(slopes, axis=1), jnp.concatenate(ks, axis=0)) * 0.125
            dp_s[rows, p * BLOCK : (p + 1) * BLOCK] = dq.astype(low)
            dp_s[rows, width + p * BLOCK : width + (p + 1) * BLOCK] = dk.astype(low)
            dp_s[rows, 2 * width + p * BLOCK : 2 * width + (p + 1) * BLOCK] = dv.astype(low)
    sq[...] += fold_rows(dp_s[...].astype(full))
    for n0, n1 in column_blocks(3 * width, 512):
        accq[:, n0:n1] += nn(xt_s[...], dp_s[:, n0:n1])
    if layer:
        input_gradient(
            scal_ref, layer, x_ref, dres_ref, dp_s, wqkv, vec, None, (result_ref,), dna_s
        )

    @pl.when(pl.program_id(0) == pl.num_programs(0) - 1)
    def _():
        small = small_block([sq[...]])

        def write(ref, h):
            base = store_columns(ref, 0, accq, h * width // 2, width // 2)
            store_rest(ref, base, small)

        store_payload(scal_ref, keep_ref, send_ref, write)


def call_kernel(
    kernel, scal, steps, blocked, fixed, hbm, outs, fixed_outs, scratch, flops, moved, fuse=False
):
    own_index = lambda i, s: (i, 0)
    shared_index = lambda i, s: (s[0] * steps + i, 0)

    def spec(shape, shared):
        rows = shape[0] // (2 * steps if shared else steps)
        return pl.BlockSpec((rows, shape[1]), shared_index if shared else own_index)

    in_specs, args = [], []
    for array, shared in blocked:
        in_specs.append(spec(array.shape, shared))
        args.append(array)
    for array in fixed:
        in_specs.append(pl.BlockSpec(array.shape, lambda i, s, n=array.ndim: (0,) * n))
        args.append(array)
    for array in hbm:
        in_specs.append(pl.BlockSpec(memory_space=pl.ANY))
        args.append(array)
    out_specs, out_shapes = [], []
    for shape, dtype, shared in outs:
        out_specs.append(spec(shape, shared))
        out_shapes.append(jax.ShapeDtypeStruct(shape, dtype))
    for shape, dtype in fixed_outs:
        out_specs.append(pl.BlockSpec(shape, lambda i, s, n=len(shape): (0,) * n))
        out_shapes.append(jax.ShapeDtypeStruct(shape, dtype))
    return pl.pallas_call(
        kernel,
        grid_spec=pltpu.PrefetchScalarGridSpec(
            num_scalar_prefetch=1,
            grid=(steps,),
            in_specs=in_specs,
            out_specs=out_specs,
            scratch_shapes=scratch,
        ),
        out_shape=out_shapes,
        compiler_params=pltpu.CompilerParams(
            vmem_limit_bytes=VMEM_LIMIT, fuse_transposed_lhs_in_matmul=fuse
        ),
        cost_estimate=pl.CostEstimate(flops=flops, bytes_accessed=moved, transcendentals=0),
    )(scal, *args)


def run_forward(layer, scal, x, shared, segments, pad, own, other, tokens, slots):
    width = x.shape[1]
    hidden_width = own[2].shape[1]
    steps = tokens // (R_F * slots)
    per_step = R_F * slots
    if layer == 0:
        outs = [((tokens, width), low, False)]
    else:
        outs = [((tokens, width), low, False), ((2 * tokens, width), low, True)]
    outs += [
        ((tokens, 3 * width), low, False),
        ((tokens, H * slots), low, False),
        ((tokens, width), full, False),
        ((tokens, width), low, False),
        ((tokens, width), low, False),
        ((tokens, BLOCK), full, False),
        ((tokens, hidden_width), low, False),
        ((tokens, hidden_width), low, False),
    ]
    scratch = [pltpu.VMEM(w.shape, w.dtype) for w in own] + [
        pltpu.VMEM((per_step, width), low),
        pltpu.VMEM((per_step, width), full),
        pltpu.VMEM((per_step, width), low),
        pltpu.VMEM((per_step, BLOCK), low),
        pltpu.VMEM((per_step, BLOCK), low),
        pltpu.VMEM((per_step, BLOCK), full),
        pltpu.SemaphoreType.DMA((5,)),
    ]
    return call_kernel(
        functools.partial(forward_kernel, layer, slots),
        scal,
        steps,
        [(x, shared)],
        [segments, pad],
        list(own) + list(other),
        outs,
        [],
        scratch,
        2 * tokens * (4 * width * width + 2 * width * hidden_width + 2 * slots * width),
        tokens * 14000,
    )


def payload_rows(used, devices):
    unit = devices * 16
    return -(-used // unit) * unit


def run_ffn_backward(layer, scal, dy, shared, pad, saved, own, other, tokens, slots, devices):
    width, hidden_width = own[0].shape
    steps = tokens // (R_FB * slots)
    per_step = R_FB * slots
    rows = payload_rows((hidden_width + width // 2) * width // BLOCK + 32, devices)
    scratch = [pltpu.VMEM(w.shape, w.dtype) for w in own] + [
        pltpu.VMEM((per_step, width), low),
        pltpu.VMEM((width, per_step), low),
        pltpu.VMEM((width, per_step), low),
        pltpu.VMEM((width, per_step), low),
        pltpu.VMEM((per_step, hidden_width), low),
        pltpu.VMEM((per_step, width), full),
        pltpu.VMEM((width, hidden_width), full),
        pltpu.VMEM((width, hidden_width), full),
        pltpu.VMEM((width, width), full),
        pltpu.VMEM((8, hidden_width), full),
        pltpu.VMEM((8, width), full),
        pltpu.VMEM((8, width), full),
        pltpu.SemaphoreType.DMA((3,)),
    ]
    return call_kernel(
        functools.partial(ffn_backward_kernel, layer, slots),
        scal,
        steps,
        [(dy, shared)] + [(array, False) for array in saved],
        [pad],
        list(own) + list(other),
        [((tokens, width), full, False)],
        [((rows, BLOCK), low), ((rows, BLOCK), low)],
        scratch,
        8 * tokens * width * hidden_width,
        tokens * 10000,
    )


def run_attention_backward(layer, scal, x, shared, saved, own, other, tokens, slots, devices):
    width = x.shape[1]
    steps = tokens // (R_AB * slots)
    per_step = R_AB * slots
    rows = payload_rows(3 * width * width // 2 // BLOCK + 16, devices)
    blocked = [(x, shared)] + [(array, False) for array in saved]
    result_width = width if layer else 3 * width
    scratch = [pltpu.VMEM(w.shape, w.dtype) for w in own] + [
        pltpu.VMEM((per_step, width), low),
        pltpu.VMEM((per_step, width), low),
        pltpu.VMEM((per_step, width), low),
        pltpu.VMEM((width, per_step), low),
        pltpu.VMEM((per_step, width), full),
    ]
    if layer:
        scratch.append(pltpu.VMEM((per_step, 3 * width), low))
    scratch += [
        pltpu.VMEM((width, 3 * width), full),
        pltpu.VMEM((8, 3 * width), full),
        pltpu.SemaphoreType.DMA((3,)),
    ]
    return call_kernel(
        functools.partial(attention_backward_kernel, layer, slots),
        scal,
        steps,
        blocked,
        [],
        list(own) + list(other),
        [((tokens, result_width), low, False)],
        [((rows, BLOCK), low), ((rows, BLOCK), low)],
        scratch,
        2 * tokens * (8 * width * width + 5 * slots * width),
        tokens * 11000,
        fuse=True,
    )


def run_input_gradient(layer, scal, x, dres, dproj, later, own, other, tokens, slots):
    width = x.shape[1]
    steps = tokens // (R_AB * slots)
    per_step = R_AB * slots
    scratch = [pltpu.VMEM(w.shape, w.dtype) for w in own] + [
        pltpu.VMEM((per_step, width), full),
        pltpu.SemaphoreType.DMA((2,)),
    ]
    return call_kernel(
        functools.partial(input_gradient_kernel, layer),
        scal,
        steps,
        [(x, True), (dres, False), (dproj, False), (later, False)],
        [],
        list(own) + list(other),
        [((tokens, width), low, False), ((2 * tokens, width), full, True)],
        [],
        scratch,
        6 * tokens * width * width,
        tokens * 7000,
    )


def fill_kernel(scal_ref, got_ref, held_ref, out_ref):
    del scal_ref, held_ref
    out_ref[...] = got_ref[...].astype(out_ref.dtype)


def fill_other_half(scal, held, got, steps):
    rows = got.shape[0] // steps
    return pl.pallas_call(
        fill_kernel,
        grid_spec=pltpu.PrefetchScalarGridSpec(
            num_scalar_prefetch=1,
            grid=(steps,),
            in_specs=[
                pl.BlockSpec((rows, got.shape[1]), lambda i, s: (i, 0)),
                pl.BlockSpec(memory_space=pl.ANY),
            ],
            out_specs=pl.BlockSpec(
                (rows, got.shape[1]), lambda i, s: ((1 - s[0]) * steps + i, 0)
            ),
        ),
        out_shape=jax.ShapeDtypeStruct(held.shape, held.dtype),
        input_output_aliases={2: 0},
        cost_estimate=pl.CostEstimate(
            flops=0, bytes_accessed=8 * got.size, transcendentals=0
        ),
    )(scal, got, held)


def single_step(kernel, scal, arrays, shapes, scratch=()):
    whole = lambda shape: pl.BlockSpec(shape, lambda i, s, n=len(shape): (0,) * n)
    moved = sum(a.size * a.dtype.itemsize for a in arrays)
    return pl.pallas_call(
        kernel,
        grid_spec=pltpu.PrefetchScalarGridSpec(
            num_scalar_prefetch=1,
            grid=(1,),
            in_specs=[whole(a.shape) for a in arrays],
            out_specs=[whole(shape) for shape, _ in shapes],
            scratch_shapes=list(scratch),
        ),
        out_shape=[jax.ShapeDtypeStruct(shape, dtype) for shape, dtype in shapes],
        compiler_params=pltpu.CompilerParams(vmem_limit_bytes=VMEM_LIMIT),
        cost_estimate=pl.CostEstimate(flops=0, bytes_accessed=3 * moved, transcendentals=0),
    )(scal, *arrays)


def turned_row(row):
    return jnp.broadcast_to(row, (BLOCK, row.shape[1])).T


def small_rows(block, row, size):
    return jnp.concatenate([block[row + j : row + j + 1, :] for j in range(size // BLOCK)], axis=1)


def finish_normed(source, base, h, sums, gain, shift, weight, out_ref, parts_ref):
    rows = weight.shape[0] // 2
    half = slice(h * rows, (h + 1) * rows)
    for b in range(weight.shape[1] // BLOCK):
        cols = slice(b * BLOCK, (b + 1) * BLOCK)
        value = source[base + b * rows : base + (b + 1) * rows, :].astype(full)
        out_ref[0, half, cols] = gain[half, :] * value + shift[half, :] * sums[:, cols]
        parts_ref[half, cols] = value * weight[half, cols].astype(full)
    return base + rows * (weight.shape[1] // BLOCK)


def row_sums(parts, weight, sums):
    ones = jnp.ones((16, parts.shape[1]), low)
    high = parts.astype(low)
    rest = (parts - high.astype(full)).astype(low)
    first = nt(ones, high) + nt(ones, rest)
    wide = jnp.broadcast_to(sums, (16, sums.shape[1]))
    high = wide.astype(low)
    rest = (wide - high.astype(full)).astype(low)
    second = nt(high, weight) + nt(rest, weight)
    return first[0:1, :], second[0:1, :]


def unpack_ffn_kernel(
    scal_ref, first, second, got, wup, vec, down, up, out, up_b, down_b, out_b, gain_g, shift_g, parts
):
    width, hidden_width = wup.shape
    matrices = (hidden_width // 2) * (width // BLOCK)
    base_small = 2 * matrices + (width // 2) * (width // BLOCK)
    small = got[base_small : base_small + 32, :].astype(full)
    sums = small_rows(small, 0, hidden_width)
    gain, shift = turned_row(vec[5:6, :]), turned_row(vec[6:7, :])

    def write(source, h):
        half = hidden_width // 2
        for b in range(width // BLOCK):
            down[0, h * half : (h + 1) * half, b * BLOCK : (b + 1) * BLOCK] = source[
                b * half : (b + 1) * half, :
            ].astype(full)
        base = finish_normed(source, matrices, h, sums, gain, shift, wup, up, parts)
        half = width // 2
        for b in range(width // BLOCK):
            out[0, h * half : (h + 1) * half, b * BLOCK : (b + 1) * BLOCK] = source[
                base + b * half : base + (b + 1) * half, :
            ].astype(full)

    @pl.when(scal_ref[0] == 0)
    def _():
        write(first, 0)
        write(got, 1)

    @pl.when(scal_ref[0] != 0)
    def _():
        write(got, 0)
        write(second, 1)

    up_b[...] = sums
    row = hidden_width // BLOCK
    down_b[...] = small_rows(small, row, width)
    out_b[...] = small_rows(small, row + width // BLOCK, width)
    gain_g[...], shift_g[...] = row_sums(parts[...], wup[...], sums)


def unpack_attention_kernel(
    scal_ref, chunks, wqkv, vec, grad, qv_b, gain_g, shift_g, halves, parts
):
    del scal_ref
    width = wqkv.shape[0]
    count, rows = chunks.shape[0], chunks.shape[1] // 2
    for j in range(count):
        for h in range(2):
            halves[h, j * rows : (j + 1) * rows, :] = chunks[j, h * rows : (h + 1) * rows, :]
    base_small = (width // 2) * (3 * width // BLOCK)
    small = halves[0, base_small : base_small + 16, :].astype(full)
    sums = small_rows(small, 0, 3 * width)
    gain, shift = turned_row(vec[0:1, :]), turned_row(vec[1:2, :])
    for h in range(2):
        finish_normed(halves.at[h], 0, h, sums, gain, shift, wqkv, grad, parts)
    qv_b[:, :width] = sums[:, :width]
    qv_b[:, width:] = sums[:, 2 * width :]
    gain_g[...], shift_g[...] = row_sums(parts[...], wqkv[...], sums)


SWAP = [(0, 1), (1, 0)]


def scatter_blocks(array, devices):
    return lax.all_to_all(array.reshape(devices, -1, BLOCK), "dp", 0, 0)


def gather_blocks(array, devices):
    return lax.all_to_all(jnp.broadcast_to(array[None], (devices,) + array.shape), "dp", 0, 0)


def add_up(blocks):
    return jnp.sum(blocks.astype(full), axis=0).astype(low)


def pair_sum(keep, send):
    got = lax.ppermute(send, "section", SWAP)
    return (keep.astype(full) + got.astype(full)).astype(low)


together = lax.optimization_barrier


def per_device(
    activations,
    cotangent,
    segment_ids,
    pad_mask,
    norm1_gain,
    norm1_bias,
    qkv_weight,
    qv_bias,
    out_weight,
    out_bias,
    norm2_gain,
    norm2_bias,
    up_weight,
    up_bias,
    down_weight,
    down_bias,
):
    devices = lax.axis_size("dp")
    scal = lax.axis_index("section").astype(jnp.int32).reshape(1)
    local_rows, slots, width = activations.shape
    hidden_width = up_weight.shape[-1]
    tokens = local_rows // 2 * slots

    vec_rows = 8 + hidden_width // width
    vec = pl.pallas_call(
        pack_kernel, out_shape=jax.ShapeDtypeStruct((vec_rows, width), full)
    )(norm1_gain, norm1_bias, qv_bias, out_bias, norm2_gain, norm2_bias, up_bias, down_bias)
    own = (qkv_weight[0], out_weight[0], up_weight[0], down_weight[0], vec)
    other = tuple(lax.ppermute(w, "section", SWAP) for w in own)
    attn_own, attn_other = (own[0], own[1], own[4]), (other[0], other[1], other[4])
    ffn_own, ffn_other = own[2:], other[2:]

    x = activations.reshape(-1, width)
    seed = cotangent.reshape(-1, width)

    first, *kept1 = run_forward(
        0, scal, x, True, segment_ids, pad_mask, own, other, tokens, slots
    )
    outs_send, outs_mine, *kept2 = run_forward(
        1, scal, first, False, segment_ids, pad_mask, own, other, tokens, slots
    )
    outs_got = lax.ppermute(outs_send, "section", SWAP)

    dres2, ffn2_keep, ffn2_send = run_ffn_backward(
        1, scal, seed, True, pad_mask, kept2[3:], ffn_own, ffn_other, tokens, slots, devices
    )
    ffn2 = pair_sum(ffn2_keep, ffn2_send)
    dres2, ffn2 = together((dres2, ffn2))
    ffn2 = lax.psum(ffn2, "dp")
    dx2, attn2_keep, attn2_send = run_attention_backward(
        1, scal, first, False, [dres2] + kept2[:4], attn_own, attn_other, tokens, slots, devices
    )
    attn2 = pair_sum(attn2_keep, attn2_send)
    dx2, attn2 = together((dx2, attn2))
    attn2 = scatter_blocks(attn2, devices)
    dres1, ffn1_keep, ffn1_send = run_ffn_backward(
        0, scal, dx2, False, pad_mask, kept1[3:], ffn_own, ffn_other, tokens, slots, devices
    )
    dres1, ffn1_keep, ffn1_send, attn2 = together((dres1, ffn1_keep, ffn1_send, attn2))
    ffn1 = pair_sum(ffn1_keep, ffn1_send)
    dres1, ffn1, attn2 = together((dres1, ffn1, add_up(attn2)))
    ffn1 = scatter_blocks(ffn1, devices)
    dproj, attn1_keep, attn1_send = run_attention_backward(
        0, scal, x, True, [dres1] + kept1[:4], attn_own, attn_other, tokens, slots, devices
    )
    attn1 = pair_sum(attn1_keep, attn1_send)
    dproj, attn1 = together((dproj, attn1))
    attn1 = scatter_blocks(attn1, devices)
    grads_send, grads_mine = run_input_gradient(
        0, scal, x, dres1, dproj, dx2, (own[0], own[4]), (other[0], other[4]), tokens, slots
    )
    grads_send, grads_mine, ffn1, attn1 = together((grads_send, grads_mine, ffn1, attn1))
    is_first = scal[0] == 0
    ffn1 = gather_blocks(add_up(ffn1), devices)
    attn1 = add_up(attn1)
    got = lax.ppermute(jnp.where(is_first, attn2, attn1), "section", SWAP)
    chunk = jnp.concatenate(
        [jnp.where(is_first, attn1, got), jnp.where(is_first, got, attn2)], axis=0
    )
    attn = gather_blocks(chunk, devices)
    grads_got = lax.ppermute(grads_send, "section", SWAP)
    layer_outs = fill_other_half(scal, outs_mine, outs_got, 4)
    layer_in_grads = fill_other_half(scal, grads_mine, grads_got, 4)
    ffn1, attn, layer_outs, layer_in_grads = together((ffn1, attn, layer_outs, layer_in_grads))

    ffn1 = ffn1.reshape(-1, BLOCK)
    got = lax.ppermute(jnp.where(is_first, ffn2, ffn1), "section", SWAP)
    row = ((1, width), full)
    qkv_grad, qv_b, gain1, shift1 = single_step(
        unpack_attention_kernel,
        scal,
        [attn, own[0], vec],
        [((1, width, 3 * width), full), ((1, 2 * width), full), row, row],
        [
            pltpu.VMEM((2, devices * chunk.shape[0] // 2, BLOCK), low),
            pltpu.VMEM((width, 3 * width), full),
        ],
    )
    down_grad, up_grad, out_grad, up_b, down_b, out_b, gain2, shift2 = single_step(
        unpack_ffn_kernel,
        scal,
        [ffn1, ffn2, got, own[2], vec],
        [
            ((1, hidden_width, width), full),
            ((1, width, hidden_width), full),
            ((1, width, width), full),
            ((1, hidden_width), full),
            row,
            row,
            row,
            row,
        ],
        [pltpu.VMEM((width, hidden_width), full)],
    )
    shape = (1, local_rows, slots, width)
    return (
        layer_outs.reshape(shape),
        layer_in_grads.reshape(shape),
        gain1,
        shift1,
        qkv_grad,
        qv_b,
        out_grad,
        out_b,
        gain2,
        shift2,
        up_grad,
        up_b,
        down_grad,
        down_b,
    )


def solution(mesh):
    in_specs = (
        P("dp", None, None),
        P("dp", None, None),
        P("dp", None),
        P("dp", None),
        P("section", None),
        P("section", None),
        P("section", None, None),
        P("section", None),
        P("section", None, None),
        P("section", None),
        P("section", None),
        P("section", None),
        P("section", None, None),
        P("section", None),
        P("section", None, None),
        P("section", None),
    )
    out_specs = (
        P("section", "dp", None, None),
        P("section", "dp", None, None),
        P("section", None),
        P("section", None),
        P("section", None, None),
        P("section", None),
        P("section", None, None),
        P("section", None),
        P("section", None),
        P("section", None),
        P("section", None, None),
        P("section", None),
        P("section", None, None),
        P("section", None),
    )
    return jax.shard_map(
        per_device, mesh=mesh, in_specs=in_specs, out_specs=out_specs, check_vma=False
    )
```
